32 devices in a mesh: grp: 2 (over y), tx: 4 (over z), ty: 4 (over x, core).
Axes of the slice: x: 2, y: 2, z: 4, core: 2. Of those that a mesh axis runs over, the one named last changes fastest.
Arguments:
- cell_current: float32 [4096, 512], P(('grp', 'tx'), 'ty'), parts along dimension 0, may hold values from -48 to 48
- block_row: int32 [4096], P(('grp', 'tx')), parts along dimension 0, may hold values from 0 to 255
- block_count: int32 [8], P(('grp', 'tx')), parts along dimension 0, may hold values from 128 to 512, as said below
- cond_x: float32 [4, 512, 512], P(None, ('grp', 'tx'), 'ty'), parts along dimension 1, may hold values from 0.5 to 8
- cond_y: float32 [4, 512, 512], P(None, ('grp', 'tx'), 'ty'), parts along dimension 1, may hold values from 0.5 to 8
- cond_via: float32 [3, 512, 512], P(None, ('grp', 'tx'), 'ty'), parts along dimension 1, may hold values from 0.5 to 8
- ground: float32 [4, 512, 512], P(None, ('grp', 'tx'), 'ty'), parts along dimension 1, may hold values from 0.5 to 4
- drop_weight: float32 [4, 512, 512], P(None, ('grp', 'tx'), 'ty'), parts along dimension 1, may hold values from -48 to 48
Outputs:
- drop: float32 [4, 512, 512], P(None, ('grp', 'tx'), 'ty'), parts along dimension 1
- cell_sense: float32 [4096, 512], P(('grp', 'tx'), 'ty'), parts along dimension 0
The draws below stay inside these ranges and needn't reach their ends.
There are 2 independent parts, one for each index of `grp`. The reference program is written for one: setup_inputs(seed, part) draws one part's arguments, and reference() takes and returns one part's arrays. A program takes and returns all parts, laid end to end along the dimension named above; each array names one. Nothing has to cross between parts.
Inputs may be any that keep to these rules, and one draw needn't show every extreme that they name: `block_count`: every live count is at least a quarter of 512; in every draw some index of tx has all 512 blocks live.
All inputs are finite; a program needn't handle non-finite values.
Results may differ from the reference program's by a relative error of at most 0.00013.
Values sent between devices are 32-bit elements; how exact they have to be, the bound alone decides.
No kernel may reach another device: no remote copies, remote signals or barrier semaphores. Data moves between devices by JAX's collectives and lax.ppermute only.
A program may use at most 64 MiB of HBM per device.

```python
import math
import jax
import jax.numpy as jnp

LAYERS = 4
BLK_DEV = 512
ITERS = 2
SWEEPS = 2
NX = 256
NY = 512
BLOCKS = 2048
N_TX = 4


def draw_block_count(key, part):
    key = jax.random.fold_in(key, 7)
    first_key, second_key = jax.random.split(key)
    counts = jax.random.randint(first_key, (N_TX,), BLK_DEV // 4, BLK_DEV + 1, dtype=jnp.int32)
    chosen = jax.random.randint(second_key, (), 0, N_TX, dtype=jnp.int32)
    return jnp.where(jnp.arange(N_TX, dtype=jnp.int32) == chosen, BLK_DEV, counts).astype(jnp.int32)


def touch_ends(array, stream_key, low, top_value):
    shape = array.shape
    spot = [jax.random.randint(jax.random.fold_in(stream_key, axis), (), 0, shape[axis]) for axis in range(len(shape))]
    array = array.at[tuple(spot)].set(low)
    longest = shape.index(max(shape))
    spot[longest] = (spot[longest] + 1) % shape[longest]
    return array.at[tuple(spot)].set(top_value)


def block_levels(rng, extent, cuts, least, largest):
    level, own = 1.0, jax.random.fold_in(rng, 6)
    for axis_at, blocks in cuts:
        heights = jnp.exp(jax.random.uniform(jax.random.fold_in(own, axis_at), (blocks,), jnp.float32, least / len(cuts), largest / len(cuts)))
        level = level * jnp.repeat(heights, extent[axis_at] // blocks).reshape([-1 if axis == axis_at else 1 for axis in range(len(extent))])
    return level


def normal_values(key, extent, width, bound, shards=(), kind=jnp.bfloat16):
    result = jax.random.normal(key, extent, jnp.float32) * width
    if len(shards) > 0:
        result = block_levels(key, extent, shards, -0.22, 0.18) * result
    return jnp.clip(result, min=-bound, max=bound).astype(kind)


def setup_inputs(seed: int = 0, part: int = 0) -> dict:
    seeds = jax.random.split(jax.random.key(seed), 9)
    own_keys = jax.random.split(jax.random.fold_in(seeds[8], part), 9)
    cell_current = normal_values(own_keys[0], (BLOCKS, NY), 8.0, 48.0, ((0, 4), (1, 4)), jnp.float32)
    block_row = touch_ends(jax.random.randint(own_keys[1], (BLOCKS,), 0, NX), jax.random.fold_in(own_keys[1], 1), 0, NX - 1).astype(jnp.int32)
    block_count = draw_block_count(jax.random.fold_in(jax.random.fold_in(seeds[8], part), 71), part)
    cond_x = jnp.clip(jnp.exp(math.log(8.0) - 2.7725887 * jax.random.uniform(own_keys[3], (LAYERS, NX, NY), jnp.float32) ** block_levels(own_keys[3], (LAYERS, NX, NY), ((1, 4), (2, 4)), -0.2, 0.2)), 0.5, 8.0)
    cond_y = jnp.clip(jnp.exp(math.log(8.0) - 2.7725887 * jax.random.uniform(own_keys[4], (LAYERS, NX, NY), jnp.float32) ** block_levels(own_keys[4], (LAYERS, NX, NY), ((1, 4), (2, 4)), -0.2, 0.2)), 0.5, 8.0)
    cond_via = jnp.clip(jnp.exp(math.log(8.0) - 2.7725887 * jax.random.uniform(own_keys[5], (LAYERS - 1, NX, NY), jnp.float32) ** block_levels(own_keys[5], (LAYERS - 1, NX, NY), ((1, 4), (2, 4)), -0.2, 0.2)), 0.5, 8.0)
    ground = jnp.clip(jnp.exp(math.log(4.0) - 2.0794415 * jax.random.uniform(own_keys[6], (LAYERS, NX, NY), jnp.float32) ** block_levels(own_keys[6], (LAYERS, NX, NY), ((1, 4), (2, 4)), -0.2, 0.2)), 0.5, 4.0)
    drop_weight = normal_values(own_keys[7], (LAYERS, NX, NY), 8.0, 48.0, ((1, 4), (2, 4)), jnp.float32)
    return {"cell_current": cell_current, "block_row": block_row, "block_count": block_count, "cond_x": cond_x, "cond_y": cond_y, "cond_via": cond_via, "ground": ground, "drop_weight": drop_weight}


def operate(v, cond_x, cond_y, cond_via, ground):
    zx = jnp.zeros((v.shape[0], 1, v.shape[2]), jnp.float32)
    fx = cond_x * (v - jnp.concatenate([v[:, 1:], zx], 1))
    fx_low = jnp.concatenate([zx, fx[:, :-1]], 1)
    zy = jnp.zeros((v.shape[0], v.shape[1], 1), jnp.float32)
    fy = cond_y * (v - jnp.concatenate([v[:, :, 1:], zy], 2))
    fy_low = jnp.concatenate([zy, fy[:, :, :-1]], 2)
    zl = jnp.zeros((1, v.shape[1], v.shape[2]), jnp.float32)
    fz = cond_via * (v[:-1] - v[1:])
    vertical = jnp.concatenate([fz, zl], 0) - jnp.concatenate([zl, fz], 0)
    return ground * v + (fx - fx_low) + (fy - fy_low) + vertical


def solve(rhs, cond_x, cond_y, cond_via, ground, inverse):
    def apply(v):
        return operate(v, cond_x, cond_y, cond_via, ground)

    def precondition(resid):
        guess = inverse * resid
        for sweep in range(SWEEPS - 1):
            guess = guess + inverse * (resid - apply(guess))
        return guess

    solution = jnp.zeros_like(rhs)
    resid = rhs
    zvec = precondition(resid)
    direction = zvec
    rz_now = jnp.sum(resid * zvec)
    for step in range(ITERS):
        image = apply(direction)
        alpha = rz_now / jnp.sum(direction * image)
        solution = solution + alpha * direction
        resid = resid - alpha * image
        if step + 1 < ITERS:
            zvec = precondition(resid)
            rz_next = jnp.sum(resid * zvec)
            direction = zvec + (rz_next / rz_now) * direction
            rz_now = rz_next
    return solution


def reference(cell_current, block_row, block_count, cond_x, cond_y, cond_via, ground, drop_weight):
    live = (jnp.arange(BLK_DEV, dtype=jnp.int32)[None, :] < block_count[:, None]).reshape(-1)
    weighted = jnp.where(live[:, None], cell_current, 0.0).astype(jnp.float32)
    source = jnp.zeros((NX, NY), jnp.float32).at[block_row].add(weighted)
    rhs = jnp.zeros((LAYERS, NX, NY), jnp.float32).at[0].set(source)
    zx = jnp.zeros((LAYERS, 1, NY), jnp.float32)
    zy = jnp.zeros((LAYERS, NX, 1), jnp.float32)
    zl = jnp.zeros((1, NX, NY), jnp.float32)
    diagonal = ground + cond_x + jnp.concatenate([zx, cond_x[:, :-1]], 1) + cond_y + jnp.concatenate([zy, cond_y[:, :, :-1]], 2) + jnp.concatenate([cond_via, zl], 0) + jnp.concatenate([zl, cond_via], 0)
    inverse = 1.0 / diagonal
    drop = solve(rhs, cond_x, cond_y, cond_via, ground, inverse)
    adjoint = solve(drop_weight, cond_x, cond_y, cond_via, ground, inverse)
    cell_sense = jnp.where(live[:, None], adjoint[0][block_row], 0.0).astype(jnp.float32)
    return drop, cell_sense
```

```python
import functools

import jax
import jax.numpy as jnp
from jax import lax
from jax.experimental import pallas as pl
from jax.experimental.pallas import tpu as pltpu
from jax.sharding import PartitionSpec as P

HALO = 4
SUB = 8
LANES = 128
SLOTS = LANES // HALO
PAIRS = LANES // (2 * HALO)
F32 = jnp.float32
BF16 = jnp.bfloat16


def lanes_of(shape):
    return lax.broadcasted_iota(jnp.int32, shape, len(shape) - 1)


def rows_of(shape):
    return lax.broadcasted_iota(jnp.int32, shape, len(shape) - 2)


def tiles_of(refs):
    found = []
    for ref in refs:
        rows = ref.shape[-2]
        for plane in range(ref.shape[0] if len(ref.shape) == 3 else 1):
            for at in range(0, rows, SUB):
                if len(ref.shape) == 3:
                    found.append((ref, (plane, slice(at, at + SUB), slice(None))))
                else:
                    found.append((ref, (slice(at, at + SUB), slice(None))))
    return found


def three_parts(value):
    high = value.astype(BF16)
    rest = value - high.astype(F32)
    middle = rest.astype(BF16)
    low = (rest - middle.astype(F32)).astype(BF16)
    return high, middle, low


def dot(left, right):
    return jnp.dot(left, right, preferred_element_type=F32)


def pack_columns(cx, cy, via, ground, weight, cell, to_right, to_left):
    slot = lanes_of((SUB, LANES)) // HALO
    tiles = tiles_of((cx, cy, via, ground, weight, cell))
    for first in range(0, len(tiles), SLOTS):
        left = jnp.zeros((SUB, LANES), F32)
        right = left
        for s, (ref, index) in enumerate(tiles[first : first + SLOTS]):
            turned = pltpu.roll(ref[index], HALO * s, 1) if s else ref[index]
            left = jnp.where(slot == s, turned, left)
            right = jnp.where(slot == (s - 1) % SLOTS, turned, right)
        at = first // SLOTS * SUB
        to_right[at : at + SUB, :] = right
        to_left[at : at + SUB, :] = left


def pick(count, rows, block_row, block_count, cell, picker, chooser, main):
    me = lax.axis_index("tx")
    blocks = block_row.shape[1]
    ring = rows + 2 * HALO
    at = block_row[...]
    live = lanes_of((1, blocks)) < block_count[0]
    at = jnp.where(live, at, -rows)
    line = rows_of((ring, blocks))
    line = jnp.where(line < rows + HALO, line, line - ring)
    for k in range(count):
        owner = lax.rem(me + k, count) * rows
        hot = (line == at - owner).astype(F32)
        picker[k * ring : (k + 1) * ring, :] = hot
        owner = lax.rem(me - k + count, count) * rows
        hot = (rows_of((rows, blocks)) == at - owner).astype(F32)
        chooser[:, k * rows : (k + 1) * rows] = hot.T.astype(BF16)
    high, middle, low = three_parts(cell[...])
    hot = picker[...].astype(BF16)
    main[...] = dot(hot, high) + dot(hot, middle) + dot(hot, low)


def assemble(count, shape, refs):
    cx, cy, via, ground, weight, from_left, from_right, picker, main = refs[:9]
    side, source = refs[9:11]
    sends = refs[11 : 11 + count - 1]
    cells = refs[-1]
    rows, ring = shape
    slot = lanes_of((SUB, LANES)) // HALO
    pair = lanes_of((SUB, LANES)) // (2 * HALO)
    lower = rows_of((SUB, LANES)) < HALO
    for j, (ref, index) in enumerate(tiles_of((side, cells))):
        q, s = divmod(j, SLOTS)
        both = jnp.where(
            slot == s, from_right[q * SUB : (q + 1) * SUB, :], from_left[q * SUB : (q + 1) * SUB, :]
        )
        ref[index] = pltpu.roll(both, LANES - HALO * s, 1) if s else both

    lane = lanes_of(cells.shape)
    edge = jnp.where((lane < HALO) | (lane >= LANES - HALO), cells[...], 0.0)
    high = edge.astype(BF16).astype(F32)
    rest = edge - high
    middle = rest.astype(BF16).astype(F32)
    low = rest - middle
    spread = high + pltpu.roll(middle, 2 * HALO, 1) + pltpu.roll(low, 4 * HALO, 1)
    sums = dot(picker[...].astype(BF16), spread.astype(BF16))
    sums = (
        sums
        + pltpu.roll(sums, LANES - 2 * HALO, 1)
        + pltpu.roll(sums, LANES - 4 * HALO, 1)
    )

    def narrow(parts):
        packed = jnp.zeros((SUB, LANES), F32)
        for s, part in enumerate(parts):
            packed = jnp.where(pair == s, pltpu.roll(part, HALO + 2 * HALO * s, 1), packed)
        return packed

    source[0] = main[0:ring, :]
    source[1] = sums[0:ring]
    for k in range(1, count):
        send = sends[k - 1]
        send[0:ring, :] = main[k * ring : (k + 1) * ring, :]
        part = sums[k * ring : (k + 1) * ring]
        send[ring : ring + SUB, :] = narrow([part[i : i + SUB] for i in range(0, ring, SUB)])

    def halves(ref_planes, take, keep):
        packed = []
        for i in range(0, len(ref_planes), 2):
            tile = ref_planes[i][take]
            if i + 1 < len(ref_planes):
                other = pltpu.roll(ref_planes[i + 1][take], HALO, 0)
                tile = jnp.where(keep, tile, other)
            packed.append(tile)
        return packed

    whole = [ref.at[p] for ref in (cx, cy, via, ground, weight) for p in range(ref.shape[0])]
    sides = [side.at[p] for p in range(side.shape[0])]
    for k, take, keep in (
        (1, (slice(rows - SUB, rows), slice(None)), ~lower),
        (count - 1, (slice(0, SUB), slice(None)), lower),
    ):
        send = sends[k - 1]
        at = ring + SUB
        for tile in halves(whole, take, keep):
            send[at : at + SUB, :] = tile
            at += SUB
        send[at : at + SUB, :] = narrow(halves(sides, take, keep))


def solve(count, layers, shape, refs):
    cx_in, cy_in, via_in, ground_in, weight_in, side, source = refs[:7]
    got = refs[7 : 7 + count - 1]
    zed, you, message = refs[7 + count - 1 : 10 + count - 1]
    ext, base, zs, qs, ts, us = refs[10 + count - 1 :]
    rows, ring = shape
    width = 2 * LANES
    pair = lanes_of((SUB, LANES)) // (2 * HALO)
    lower = rows_of((SUB, LANES)) < HALO

    def widen(packed, s):
        return pltpu.roll(packed, LANES - HALO - 2 * HALO * s, 1)

    for i in range(0, ring, SUB):
        total = source[0, i : i + SUB, :]
        for ref in got:
            total = total + ref[i : i + SUB, :]
        base[i : i + SUB, 0:LANES] = total
        s = i // SUB
        total = got[0][ring : ring + SUB, :]
        for ref in got[1:]:
            total = total + ref[ring : ring + SUB, :]
        base[i : i + SUB, LANES:] = source[1, i : i + SUB, :] + widen(total, s)

    before, after = got[0], got[count - 2]
    inputs = [ref.at[p] for ref in (cx_in, cy_in, via_in, ground_in, weight_in) for p in range(ref.shape[0])]
    planes = len(inputs)
    at_side = ring + SUB + (planes + 1) // 2 * SUB

    def halo(p, prev_tile, next_tile):
        if p % 2 == 0:
            return jnp.where(lower, next_tile, prev_tile)
        return pltpu.roll(jnp.where(lower, prev_tile, next_tile), HALO, 0)

    for p, ref in enumerate(inputs):
        ext[p, 0:rows, 0:LANES] = ref[...]
        ext[p, 0:rows, LANES:] = side[p]
        at = ring + SUB + p // 2 * SUB
        ext[p, rows:ring, 0:LANES] = halo(p, before[at : at + SUB, :], after[at : at + SUB, :])
        ext[p, rows:ring, LANES:] = halo(
            p,
            widen(before[at_side : at_side + SUB, :], p // 2),
            widen(after[at_side : at_side + SUB, :], p // 2),
        )

    def below(v):
        return pltpu.roll(v, ring - 1, 0)

    def above(v):
        return pltpu.roll(v, 1, 0)

    def right(v):
        return pltpu.roll(v, width - 1, 1)

    def left(v):
        return pltpu.roll(v, 1, 1)

    cx = [ext[p] for p in range(layers)]
    cy = [ext[layers + p] for p in range(layers)]
    via = [ext[2 * layers + p] for p in range(layers - 1)]
    ground = [ext[3 * layers - 1 + p] for p in range(layers)]
    weight = [ext[4 * layers - 1 + p] for p in range(layers)]
    row, lane = rows_of((ring, width)), lanes_of((ring, width))
    tx, ty = lax.axis_index("tx"), lax.axis_index("ty")
    inside = (
        ((row < rows) | (row >= rows + HALO) | (tx < lax.axis_size("tx") - 1))
        & ((row < rows + HALO) | (tx > 0))
        & ((lane < LANES) | (lane >= width - HALO) | ((lane < LANES + HALO) & (ty < lax.axis_size("ty") - 1)))
        & ((lane < width - HALO) | (ty > 0))
    )
    cx_low = [jnp.where((row == 0) & (tx == 0), 0.0, above(v)) for v in cx]
    cy_low = [jnp.where((lane == 0) & (ty == 0), 0.0, left(v)) for v in cy]
    diagonal, inverse = [], []
    for p in range(layers):
        total = ground[p] + cx[p] + cx_low[p] + cy[p] + cy_low[p]
        if p + 1 < layers:
            total = total + via[p]
        if p > 0:
            total = total + via[p - 1]
        diagonal.append(total)
        inverse.append(jnp.where(inside, 1.0 / total, 0.0))

    def couple(v, p):
        total = None
        if v[p] is not None:
            total = (
                cx[p] * below(v[p])
                + cx_low[p] * above(v[p])
                + cy[p] * right(v[p])
                + cy_low[p] * left(v[p])
            )
        if p + 1 < layers and v[p + 1] is not None:
            term = via[p] * v[p + 1]
            total = term if total is None else total + term
        if p > 0 and v[p - 1] is not None:
            term = via[p - 1] * v[p - 1]
            total = term if total is None else total + term
        return total

    def smooth(b):
        scaled = [None if b[p] is None else inverse[p] * b[p] for p in range(layers)]
        result = []
        for p in range(layers):
            total = couple(scaled, p)
            if total is None:
                result.append(None)
                continue
            if b[p] is not None:
                total = total + b[p]
            result.append(inverse[p] * total)
        return result

    def tile_sum(left_, right_):
        total = None
        for p in range(layers):
            if left_[p] is None or right_[p] is None:
                continue
            term = left_[p][0:rows, 0:LANES] * right_[p][0:rows, 0:LANES]
            total = term if total is None else total + term
        return jnp.sum(total, axis=0, keepdims=True)

    for which, b in enumerate(([base[...]] + [None] * (layers - 1), weight)):
        z = smooth(b)
        q = []
        for p in range(layers):
            term = couple(z, p)
            q.append(None if z[p] is None and term is None else (-term if z[p] is None else diagonal[p] * z[p] - term))
        u = smooth(q)
        flow = []
        for p in range(layers):
            term = cx[p] * below(u[p]) + cy[p] * right(u[p])
            if p + 1 < layers:
                term = term + via[p] * u[p + 1]
            flow.append(diagonal[p] * u[p] - 2.0 * term)
        at = 2 * rows + 4 * which
        message[at : at + 4, :] = jnp.concatenate(
            [tile_sum(b, z), tile_sum(z, q), tile_sum(q, u), tile_sum(u, flow)], axis=0
        )
        if which == 0:
            for p in range(layers):
                if z[p] is not None:
                    zed[p] = z[p][0:rows, 0:LANES]
                you[p] = u[p][0:rows, 0:LANES]
        else:
            message[0:rows, :] = z[0][0:rows, 0:LANES]
            message[rows : 2 * rows, :] = u[0][0:rows, 0:LANES]


def choose(count, rows, refs):
    chooser = refs[0]
    messages = refs[1 : 1 + count]
    chosen = refs[1 + count]
    hot = chooser[...]
    for half in range(2):
        field = jnp.concatenate([ref[half * rows : (half + 1) * rows, :] for ref in messages], axis=0)
        high, middle, low = three_parts(field)
        chosen[:, half * LANES : (half + 1) * LANES] = dot(hot, high) + dot(hot, middle) + dot(hot, low)


def finish(ways, refs):
    sums = refs[:ways]
    zed, you, chosen, drop, sense = refs[ways:]
    total = sums[0][...]
    for ref in sums[1:]:
        total = total + ref[...]
    total = jnp.broadcast_to(jnp.sum(total, axis=1, keepdims=True), (SUB, LANES))
    for which in range(2):
        bz, zq, qu, uw = (total[4 * which + i : 4 * which + i + 1] for i in range(4))
        ratio = qu / zq
        step = bz / zq
        second = (zq - ratio * bz) / (uw - ratio * qu)
        first = step - second * ratio
        if which == 0:
            for p in range(you.shape[0]):
                part = second * you[p]
                drop[p] = first * zed[p] + part if p < zed.shape[0] else part
        else:
            sense[...] = first * chosen[:, 0:LANES] + second * chosen[:, LANES:]


def vmem():
    return pl.BlockSpec(memory_space=pltpu.VMEM)


def call(kernel, outs, args, scratch=(), specs=None, flops=0):
    size = sum(a.size * a.dtype.itemsize for a in list(args) + list(outs))
    return pl.pallas_call(
        kernel,
        out_shape=tuple(outs),
        in_specs=specs or [vmem() for _ in args],
        out_specs=tuple(vmem() for _ in outs),
        scratch_shapes=scratch,
        cost_estimate=pl.CostEstimate(flops=flops, bytes_accessed=size, transcendentals=0),
        compiler_params=pltpu.CompilerParams(vmem_limit_bytes=48 * 1024 * 1024),
    )(*args)


def shift(value, axis, steps):
    count = lax.axis_size(axis)
    return lax.ppermute(value, axis, [(i, (i + steps) % count) for i in range(count)])


def body(cell_current, block_row, block_count, cond_x, cond_y, cond_via, ground, drop_weight):
    blocks, width = cell_current.shape
    layers, rows, _ = cond_x.shape
    count, ways = lax.axis_size("tx"), lax.axis_size("ty")
    ring = rows + 2 * HALO
    fields = (cond_x, cond_y, cond_via, ground, drop_weight)
    planes = sum(f.shape[0] for f in fields)

    def array(*dims, dtype=F32):
        return jax.ShapeDtypeStruct(dims, dtype)

    tiles = planes * rows // SUB + blocks // SUB
    packed = array(pl.cdiv(tiles, SLOTS) * SUB, LANES)
    to_right, to_left = call(pack_columns, (packed, packed), fields + (cell_current,))
    from_left = shift(to_right, "ty", 1)
    from_right = shift(to_left, "ty", -1)

    picker, chooser, main = call(
        functools.partial(pick, count, rows),
        (array(count * ring, blocks), array(blocks, count * rows, dtype=BF16), array(count * ring, width)),
        (block_row.reshape(1, blocks), block_count, cell_current),
        specs=[vmem(), pl.BlockSpec(memory_space=pltpu.SMEM), vmem()],
    )

    edges = (planes + 1) // 2 * SUB + SUB
    lengths = [ring + SUB + (edges if k in (1, count - 1) else 0) for k in range(1, count)]
    side, source, *sends = call(
        lambda *refs: assemble(count, (rows, ring), refs),
        [array(planes, rows, LANES), array(2, ring, LANES)] + [array(n, LANES) for n in lengths],
        fields + (from_left, from_right, picker, main),
        scratch=[pltpu.VMEM((blocks, LANES), F32)],
    )
    got = [shift(send, "tx", k + 1) for k, send in enumerate(sends)]

    field = pltpu.VMEM((layers, ring, 2 * LANES), F32)
    zed, you, message = call(
        lambda *refs: solve(count, layers, (rows, ring), refs),
        (array(min(2, layers), rows, LANES), array(layers, rows, LANES), array(2 * rows + SUB, LANES)),
        fields + (side, source, *got),
        scratch=[pltpu.VMEM((planes, ring, 2 * LANES), F32), pltpu.VMEM((ring, 2 * LANES), F32)] + [field] * 4,
    )
    messages = [message] + [shift(message, "tx", k) for k in range(1, count)]
    total = functools.reduce(jnp.add, [m[2 * rows :] for m in messages])
    totals = [total] + [shift(total, "ty", k) for k in range(1, ways)]
    (chosen,) = call(
        lambda *refs: choose(count, rows, refs),
        (array(blocks, 2 * LANES),),
        (chooser, *messages),
    )
    return call(
        lambda *refs: finish(ways, refs),
        (array(layers, rows, LANES), array(blocks, width)),
        (*totals, zed, you, chosen),
    )


def solution(mesh):
    placed = (
        P(("grp", "tx"), "ty"),
        P(("grp", "tx")),
        P(("grp", "tx")),
        P(None, ("grp", "tx"), "ty"),
        P(None, ("grp", "tx"), "ty"),
        P(None, ("grp", "tx"), "ty"),
        P(None, ("grp", "tx"), "ty"),
        P(None, ("grp", "tx"), "ty"),
    )
    return jax.shard_map(
        body,
        mesh=mesh,
        in_specs=placed,
        out_specs=(P(None, ("grp", "tx"), "ty"), P(("grp", "tx"), "ty")),
        check_vma=False,
    )
```

```python
import functools

import jax
import jax.numpy as jnp
from jax import lax
from jax.experimental import pallas as pl
from jax.experimental.pallas import tpu as pltpu
from jax.sharding import PartitionSpec as P

HALO = 4
SUB = 8
LANES = 128
SLOTS = LANES // HALO
F32 = jnp.float32
BF16 = jnp.bfloat16


def lanes_of(shape):
    return lax.broadcasted_iota(jnp.int32, shape, len(shape) - 1)


def rows_of(shape):
    return lax.broadcasted_iota(jnp.int32, shape, len(shape) - 2)


def tiles_of(refs):
    found = []
    for ref in refs:
        rows = ref.shape[-2]
        for plane in range(ref.shape[0] if len(ref.shape) == 3 else 1):
            for at in range(0, rows, SUB):
                if len(ref.shape) == 3:
                    found.append((ref, (plane, slice(at, at + SUB), slice(None))))
                else:
                    found.append((ref, (slice(at, at + SUB), slice(None))))
    return found


def three_parts(value):
    high = value.astype(BF16)
    rest = value - high.astype(F32)
    middle = rest.astype(BF16)
    low = (rest - middle.astype(F32)).astype(BF16)
    return high, middle, low


def dot(left, right):
    return jnp.dot(left, right, preferred_element_type=F32)


def rounds(index, count):
    even = [(i + 1) % count if i % 2 == 0 else (i - 1) % count for i in range(count)]
    odd = [(i - 1) % count if i % 2 == 0 else (i + 1) % count for i in range(count)]
    is_even = lax.rem(index, 2) == 0
    up, down = lax.rem(index + 1, count), lax.rem(index + count - 1, count)
    plan = [
        (even, jnp.where(is_even, up, down), jnp.where(is_even, up, down)),
        (odd, jnp.where(is_even, down, up), jnp.where(is_even, down, up)),
    ]
    for k in range(2, count - 1):
        target = [(i + k) % count for i in range(count)]
        plan.append((target, lax.rem(index + k, count), lax.rem(index - k + count, count)))
    return plan


def begin(count, shape, refs):
    fields, cell_in, block_row, block_count = refs[:5], refs[5], refs[6], refs[7]
    planes, own = refs[8:10]
    sends = refs[10 : 10 + count - 1]
    cell, picker, sems = refs[10 + count - 1 :]
    rows, ring = shape
    fetch_cell = pltpu.make_async_copy(cell_in, cell, sems.at[0])
    fetch_cell.start()
    fetches, at = [], 0
    for i, ref in enumerate(fields):
        part = planes.at[at : at + ref.shape[0]]
        fetches.append(pltpu.make_async_copy(ref, part, sems.at[i + 1]))
        fetches[-1].start()
        at += ref.shape[0]

    me = lax.axis_index("tx")
    even = lax.rem(me, 2) == 0
    blocks = block_row.shape[1]
    live = lanes_of((1, blocks)) < block_count[0]
    home = jnp.where(live, block_row[...], -rows)
    line = rows_of((ring, blocks))
    line = jnp.where(line < rows + HALO, line, line - ring)
    targets = [me] + [target for _, target, _ in rounds(me, count)]
    for k, target in enumerate(targets):
        picker[k * ring : (k + 1) * ring, :] = (line == home - target * rows).astype(F32)
    hot = picker[...].astype(BF16)
    fetch_cell.wait()
    high, middle, low = three_parts(cell[...])
    sums = dot(hot, high) + dot(hot, middle) + dot(hot, low)
    own[...] = sums[0:ring]
    for k, send in enumerate(sends):
        send[0:ring, :] = sums[(k + 1) * ring : (k + 2) * ring]

    for fetch in fetches:
        fetch.wait()
    lower = rows_of((SUB, LANES)) < HALO
    for p in range(0, planes.shape[0], 2):
        first = planes[p, 0:SUB, :]
        last = planes[p, rows - SUB : rows, :]
        if p + 1 < planes.shape[0]:
            first = jnp.where(lower, first, pltpu.roll(planes[p + 1, 0:SUB, :], HALO, 0))
            last = jnp.where(lower, pltpu.roll(planes[p + 1, rows - SUB : rows, :], HALO, 0), last)
        at = ring + p // 2 * SUB
        sends[0][at : at + SUB, :] = jnp.where(even, last, first)
        sends[1][at : at + SUB, :] = jnp.where(even, first, last)


def order(count, rows, block_row, block_count, own, chooser):
    me = lax.axis_index("tx")
    blocks = block_row.shape[1]
    live = lanes_of((1, blocks)) < block_count[0]
    home = jnp.where(live, block_row[...], -rows)
    line = rows_of((rows, blocks))
    for k, source in enumerate([me] + [source for _, _, source in rounds(me, count)]):
        hot = (line == home - source * rows).astype(F32)
        chooser[:, k * rows : (k + 1) * rows] = hot.T.astype(BF16)


def columns(count, shape, refs):
    planes, own = refs[:2]
    got = refs[2 : 2 + count - 1]
    base, rims, send_even, send_odd = refs[2 + count - 1 :]
    rows, ring = shape
    tx_even = lax.rem(lax.axis_index("tx"), 2) == 0
    ty_even = lax.rem(lax.axis_index("ty"), 2) == 0
    lower = rows_of((SUB, LANES)) < HALO
    for i in range(0, ring, SUB):
        total = own[i : i + SUB, :]
        for ref in got:
            total = total + ref[i : i + SUB, :]
        base[i : i + SUB, :] = total
    for p in range(0, planes.shape[0], 2):
        at = ring + p // 2 * SUB
        one, two = got[0][at : at + SUB, :], got[1][at : at + SUB, :]
        after = jnp.where(tx_even, one, two)
        before = jnp.where(tx_even, two, one)
        rims[p] = jnp.where(lower, after, before)
        if p + 1 < planes.shape[0]:
            rims[p + 1] = pltpu.roll(jnp.where(lower, before, after), HALO, 0)

    slot = lanes_of((SUB, LANES)) // HALO
    tiles = tiles_of((planes, rims, base))
    for first in range(0, len(tiles), SLOTS):
        left = jnp.zeros((SUB, LANES), F32)
        right = left
        for s, (ref, index) in enumerate(tiles[first : first + SLOTS]):
            turned = pltpu.roll(ref[index], HALO * s, 1) if s else ref[index]
            left = jnp.where(slot == s, turned, left)
            right = jnp.where(slot == (s - 1) % SLOTS, turned, right)
        at = first // SLOTS * SUB
        send_even[at : at + SUB, :] = jnp.where(ty_even, right, left)
        send_odd[at : at + SUB, :] = jnp.where(ty_even, left, right)


def solve(layers, shape, refs):
    planes, rims, middle, even, odd, zed, you, message, ext, base = refs
    rows, ring = shape
    width = 2 * LANES
    tx, ty = lax.axis_index("tx"), lax.axis_index("ty")
    ty_even = lax.rem(ty, 2) == 0

    slot = lanes_of((SUB, LANES)) // HALO
    for j, (ref, index) in enumerate(tiles_of((planes, rims, middle))):
        q, s = divmod(j, SLOTS)
        one, two = even[q * SUB : (q + 1) * SUB, :], odd[q * SUB : (q + 1) * SUB, :]
        both = jnp.where(
            slot == s, jnp.where(ty_even, one, two), jnp.where(ty_even, two, one)
        )
        both = pltpu.roll(both, LANES - HALO * s, 1) if s else both
        if ref is middle:
            base[index[0], 0:LANES] = ref[index]
            base[index[0], LANES:] = both
        else:
            at = slice(rows, ring) if ref is rims else index[1]
            ext[index[0], at, 0:LANES] = ref[index]
            ext[index[0], at, LANES:] = both

    def below(v):
        return pltpu.roll(v, ring - 1, 0)

    def above(v):
        return pltpu.roll(v, 1, 0)

    def right(v):
        return pltpu.roll(v, width - 1, 1)

    def left(v):
        return pltpu.roll(v, 1, 1)

    cx = [ext[p] for p in range(layers)]
    cy = [ext[layers + p] for p in range(layers)]
    via = [ext[2 * layers + p] for p in range(layers - 1)]
    ground = [ext[3 * layers - 1 + p] for p in range(layers)]
    weight = [ext[4 * layers - 1 + p] for p in range(layers)]
    row, lane = rows_of((ring, width)), lanes_of((ring, width))
    inside = (
        ((row < rows) | (row >= rows + HALO) | (tx < lax.axis_size("tx") - 1))
        & ((row < rows + HALO) | (tx > 0))
        & ((lane < LANES) | (lane >= width - HALO) | ((lane < LANES + HALO) & (ty < lax.axis_size("ty") - 1)))
        & ((lane < width - HALO) | (ty > 0))
    )
    cx_low = [jnp.where((row == 0) & (tx == 0), 0.0, above(v)) for v in cx]
    cy_low = [jnp.where((lane == 0) & (ty == 0), 0.0, left(v)) for v in cy]
    diagonal, inverse = [], []
    for p in range(layers):
        total = ground[p] + cx[p] + cx_low[p] + cy[p] + cy_low[p]
        if p + 1 < layers:
            total = total + via[p]
        if p > 0:
            total = total + via[p - 1]
        diagonal.append(total)
        inverse.append(jnp.where(inside, 1.0 / total, 0.0))

    def couple(v, p):
        total = None
        if v[p] is not None:
            total = (
                cx[p] * below(v[p])
                + cx_low[p] * above(v[p])
                + cy[p] * right(v[p])
                + cy_low[p] * left(v[p])
            )
        if p + 1 < layers and v[p + 1] is not None:
            term = via[p] * v[p + 1]
            total = term if total is None else total + term
        if p > 0 and v[p - 1] is not None:
            term = via[p - 1] * v[p - 1]
            total = term if total is None else total + term
        return total

    def smooth(b):
        scaled = [None if b[p] is None else inverse[p] * b[p] for p in range(layers)]
        result = []
        for p in range(layers):
            total = couple(scaled, p)
            if total is None:
                result.append(None)
                continue
            if b[p] is not None:
                total = total + b[p]
            result.append(inverse[p] * total)
        return result

    def tile_sum(left_, right_):
        total = None
        for p in range(layers):
            if left_[p] is None or right_[p] is None:
                continue
            term = left_[p][0:rows, 0:LANES] * right_[p][0:rows, 0:LANES]
            total = term if total is None else total + term
        return jnp.sum(total, axis=0, keepdims=True)

    for which, b in enumerate(([base[...]] + [None] * (layers - 1), weight)):
        z = smooth(b)
        q = []
        for p in range(layers):
            term = couple(z, p)
            q.append(None if z[p] is None and term is None else (-term if z[p] is None else diagonal[p] * z[p] - term))
        u = smooth(q)
        flow = []
        for p in range(layers):
            term = cx[p] * below(u[p]) + cy[p] * right(u[p])
            if p + 1 < layers:
                term = term + via[p] * u[p + 1]
            flow.append(diagonal[p] * u[p] - 2.0 * term)
        at = 2 * rows + 4 * which
        message[at : at + 4, :] = jnp.concatenate(
            [tile_sum(b, z), tile_sum(z, q), tile_sum(q, u), tile_sum(u, flow)], axis=0
        )
        if which == 0:
            for p in range(layers):
                if z[p] is not None:
                    zed[p] = z[p][0:rows, 0:LANES]
                you[p] = u[p][0:rows, 0:LANES]
        else:
            message[0:rows, :] = z[0][0:rows, 0:LANES]
            message[rows : 2 * rows, :] = u[0][0:rows, 0:LANES]


def choose(count, rows, refs):
    chooser = refs[0]
    messages = refs[1 : 1 + count]
    chosen = refs[1 + count]
    hot = chooser[...]
    for half in range(2):
        field = jnp.concatenate([ref[half * rows : (half + 1) * rows, :] for ref in messages], axis=0)
        high, middle, low = three_parts(field)
        chosen[:, half * LANES : (half + 1) * LANES] = dot(hot, high) + dot(hot, middle) + dot(hot, low)


def finish(ways, refs):
    sums = refs[:ways]
    zed, you, chosen, drop, sense = refs[ways:]
    total = sums[0][...]
    for ref in sums[1:]:
        total = total + ref[...]
    total = jnp.broadcast_to(jnp.sum(total, axis=1, keepdims=True), (SUB, LANES))
    for which in range(2):
        bz, zq, qu, uw = (total[4 * which + i : 4 * which + i + 1] for i in range(4))
        ratio = qu / zq
        step = bz / zq
        second = (zq - ratio * bz) / (uw - ratio * qu)
        first = step - second * ratio
        if which == 0:
            for p in range(you.shape[0]):
                part = second * you[p]
                drop[p] = first * zed[p] + part if p < zed.shape[0] else part
        else:
            sense[...] = first * chosen[:, 0:LANES] + second * chosen[:, LANES:]


def vmem():
    return pl.BlockSpec(memory_space=pltpu.VMEM)


def call(kernel, outs, args, scratch=(), specs=None, flops=0, spare=16384):
    size = sum(a.size * a.dtype.itemsize for a in list(args) + list(outs))
    return pl.pallas_call(
        kernel,
        out_shape=tuple(outs),
        in_specs=specs or [vmem() for _ in args],
        out_specs=tuple(vmem() for _ in outs),
        scratch_shapes=scratch,
        cost_estimate=pl.CostEstimate(flops=flops, bytes_accessed=size, transcendentals=0),
        compiler_params=pltpu.CompilerParams(vmem_limit_bytes=(64 * 1024 - spare) * 1024),
    )(*args)


def exchange(values, axis):
    count = lax.axis_size(axis)
    plan = rounds(lax.axis_index(axis), count)
    return [
        lax.ppermute(value, axis, list(enumerate(target)))
        for value, (target, _, _) in zip(values, plan)
    ]


def body(cell_current, block_row, block_count, cond_x, cond_y, cond_via, ground, drop_weight):
    blocks, width = cell_current.shape
    layers, rows, _ = cond_x.shape
    count, ways = lax.axis_size("tx"), lax.axis_size("ty")
    ring = rows + 2 * HALO
    shape = (rows, ring)
    fields = (cond_x, cond_y, cond_via, ground, drop_weight)
    planes = sum(f.shape[0] for f in fields)
    block_row = block_row.reshape(1, blocks)
    smem, hbm = pl.BlockSpec(memory_space=pltpu.SMEM), pl.BlockSpec(memory_space=pltpu.HBM)

    def array(*dims, dtype=F32):
        return jax.ShapeDtypeStruct(dims, dtype)

    edges = (planes + 1) // 2 * SUB
    lengths = [ring + (edges if k < 2 else 0) for k in range(count - 1)]
    held, own, *sends = call(
        lambda *refs: begin(count, shape, refs),
        [array(planes, rows, LANES), array(ring, LANES)] + [array(n, LANES) for n in lengths],
        (
            *(pltpu.with_memory_space_constraint(f, pltpu.HBM) for f in (*fields, cell_current)),
            block_row,
            block_count,
        ),
        scratch=[
            pltpu.VMEM((blocks, LANES), F32),
            pltpu.VMEM((count * ring, blocks), F32),
            pltpu.SemaphoreType.DMA((len(fields) + 1,)),
        ],
        specs=[hbm] * 6 + [vmem(), smem],
    )
    got = exchange(sends, "tx")
    (chooser,) = call(
        functools.partial(order, count, rows),
        (array(blocks, count * rows, dtype=BF16),),
        (block_row, block_count, own),
        specs=[vmem(), smem, vmem()],
    )
    packed = array(pl.cdiv(planes * (rows // SUB + 1) + ring // SUB, SLOTS) * SUB, LANES)
    middle, rims, *sends = call(
        lambda *refs: columns(count, shape, refs),
        (array(ring, LANES), array(planes, SUB, LANES), packed, packed),
        (held, own, *got),
    )
    even, odd = exchange(sends, "ty")
    zed, you, message = call(
        lambda *refs: solve(layers, shape, refs),
        (array(min(2, layers), rows, LANES), array(layers, rows, LANES), array(2 * rows + SUB, LANES)),
        (held, rims, middle, even, odd),
        scratch=[pltpu.VMEM((planes, ring, 2 * LANES), F32), pltpu.VMEM((ring, 2 * LANES), F32)],
    )
    messages = [message] + exchange([message] * (count - 1), "tx")
    total = functools.reduce(jnp.add, [m[2 * rows :] for m in messages])
    totals = [total] + exchange([total] * (ways - 1), "ty")
    (chosen,) = call(
        lambda *refs: choose(count, rows, refs),
        (array(blocks, 2 * LANES),),
        (chooser, *messages),
    )
    return call(
        lambda *refs: finish(ways, refs),
        (array(layers, rows, LANES), array(blocks, width)),
        (*totals, zed, you, chosen),
    )


def solution(mesh):
    placed = (
        P(("grp", "tx"), "ty"),
        P(("grp", "tx")),
        P(("grp", "tx")),
        P(None, ("grp", "tx"), "ty"),
        P(None, ("grp", "tx"), "ty"),
        P(None, ("grp", "tx"), "ty"),
        P(None, ("grp", "tx"), "ty"),
        P(None, ("grp", "tx"), "ty"),
    )
    return jax.shard_map(
        body,
        mesh=mesh,
        in_specs=placed,
        out_specs=(P(None, ("grp", "tx"), "ty"), P(("grp", "tx"), "ty")),
        check_vma=False,
    )
```

```python
import functools

import jax
import jax.numpy as jnp
from jax import lax
from jax.experimental import pallas as pl
from jax.experimental.pallas import tpu as pltpu
from jax.sharding import PartitionSpec as P

HALO = 4
SUB = 8
LANES = 128
SLOTS = LANES // HALO
F32 = jnp.float32
BF16 = jnp.bfloat16
ROW_TURNS = (1, 0, 2)
DATA_TURNS = (2, 0, 1)


def lanes_of(shape):
    return lax.broadcasted_iota(jnp.int32, shape, len(shape) - 1)


def rows_of(shape):
    return lax.broadcasted_iota(jnp.int32, shape, len(shape) - 2)


def tiles_of(refs):
    found = []
    for ref in refs:
        rows = ref.shape[-2]
        for plane in range(ref.shape[0] if len(ref.shape) == 3 else 1):
            for at in range(0, rows, SUB):
                if len(ref.shape) == 3:
                    found.append((ref, (plane, slice(at, at + SUB), slice(None))))
                else:
                    found.append((ref, (slice(at, at + SUB), slice(None))))
    return found


def three_parts(value):
    high = value.astype(BF16)
    rest = value - high.astype(F32)
    middle = rest.astype(BF16)
    low = (rest - middle.astype(F32)).astype(BF16)
    return high, middle, low


def dot(left, right):
    return jnp.dot(left, right, preferred_element_type=F32)


def in_turn(values, turns, back=False):
    turns = turns + tuple(range(len(turns), len(values)))
    if back:
        turns = tuple(turns.index(k) for k in range(len(values)))
    return [values[k] for k in turns]


def rounds(index, count):
    even = [(i + 1) % count if i % 2 == 0 else (i - 1) % count for i in range(count)]
    odd = [(i - 1) % count if i % 2 == 0 else (i + 1) % count for i in range(count)]
    is_even = lax.rem(index, 2) == 0
    up, down = lax.rem(index + 1, count), lax.rem(index + count - 1, count)
    plan = [
        (even, jnp.where(is_even, up, down), jnp.where(is_even, up, down)),
        (odd, jnp.where(is_even, down, up), jnp.where(is_even, down, up)),
    ]
    for k in range(2, count - 1):
        target = [(i + k) % count for i in range(count)]
        plan.append((target, lax.rem(index + k, count), lax.rem(index - k + count, count)))
    return plan


def begin(count, shape, refs):
    fields, cell_in, row_in, block_count = refs[:5], refs[5], refs[6], refs[7]
    planes, own, home = refs[8:11]
    sends = refs[11 : 11 + count - 1]
    cell, picker, block_row, sems = refs[11 + count - 1 :]
    rows, ring = shape
    fetch_row = pltpu.make_async_copy(row_in, block_row, sems.at[6])
    fetch_row.start()
    fetch_cell = pltpu.make_async_copy(cell_in, cell, sems.at[0])
    fetch_cell.start()
    fetches, at = [], 0
    for i, ref in enumerate(fields):
        part = planes.at[at : at + ref.shape[0]]
        fetches.append(pltpu.make_async_copy(ref, part, sems.at[i + 1]))
        fetches[-1].start()
        at += ref.shape[0]

    me = lax.axis_index("tx")
    even = lax.rem(me, 2) == 0
    blocks = block_row.shape[1]
    line = rows_of((ring, blocks))
    line = jnp.where(line < rows + HALO, line, line - ring)
    fetch_row.wait()
    live = lanes_of((1, blocks)) < block_count[0]
    land = jnp.where(live, block_row[...], -rows)
    home[...] = land
    targets = [me] + [target for _, target, _ in rounds(me, count)]
    for k, target in enumerate(targets):
        picker[k * ring : (k + 1) * ring, :] = (line == land - target * rows).astype(F32)
    hot = picker[...].astype(BF16)
    fetch_cell.wait()
    high, middle, low = three_parts(cell[...])
    sums = dot(hot, high) + dot(hot, middle) + dot(hot, low)
    own[...] = sums[0:ring]
    for k, send in enumerate(sends):
        send[0:ring, :] = sums[(k + 1) * ring : (k + 2) * ring]

    for fetch in fetches:
        fetch.wait()
    lower = rows_of((SUB, LANES)) < HALO
    for p in range(0, planes.shape[0], 2):
        first = planes[p, 0:SUB, :]
        last = planes[p, rows - SUB : rows, :]
        if p + 1 < planes.shape[0]:
            first = jnp.where(lower, first, pltpu.roll(planes[p + 1, 0:SUB, :], HALO, 0))
            last = jnp.where(lower, pltpu.roll(planes[p + 1, rows - SUB : rows, :], HALO, 0), last)
        at = ring + p // 2 * SUB
        sends[0][at : at + SUB, :] = jnp.where(even, last, first)
        sends[1][at : at + SUB, :] = jnp.where(even, first, last)


def order(count, rows, home, chooser):
    me = lax.axis_index("tx")
    blocks = home.shape[1]
    line = rows_of((rows, blocks))
    for k, source in enumerate(in_turn([source for _, _, source in rounds(me, count)], DATA_TURNS) + [me]):
        hot = (line == home[...] - source * rows).astype(F32)
        chooser[:, k * rows : (k + 1) * rows] = hot.T.astype(BF16)


def columns(count, shape, refs):
    planes, own = refs[:2]
    got = in_turn(refs[2 : 2 + count - 1], ROW_TURNS, True)
    base, rims, send_even, send_odd = refs[2 + count - 1 :]
    rows, ring = shape
    tx_even = lax.rem(lax.axis_index("tx"), 2) == 0
    ty_even = lax.rem(lax.axis_index("ty"), 2) == 0
    lower = rows_of((SUB, LANES)) < HALO
    for i in range(0, ring, SUB):
        total = own[i : i + SUB, :]
        for ref in got:
            total = total + ref[i : i + SUB, :]
        base[i : i + SUB, :] = total
    for p in range(0, planes.shape[0], 2):
        at = ring + p // 2 * SUB
        one, two = got[0][at : at + SUB, :], got[1][at : at + SUB, :]
        after = jnp.where(tx_even, one, two)
        before = jnp.where(tx_even, two, one)
        rims[p] = jnp.where(lower, after, before)
        if p + 1 < planes.shape[0]:
            rims[p + 1] = pltpu.roll(jnp.where(lower, before, after), HALO, 0)

    slot = lanes_of((SUB, LANES)) // HALO
    tiles = tiles_of((planes, rims, base))
    for first in range(0, len(tiles), SLOTS):
        left = jnp.zeros((SUB, LANES), F32)
        right = left
        for s, (ref, index) in enumerate(tiles[first : first + SLOTS]):
            turned = pltpu.roll(ref[index], HALO * s, 1) if s else ref[index]
            left = jnp.where(slot == s, turned, left)
            right = jnp.where(slot == (s - 1) % SLOTS, turned, right)
        at = first // SLOTS * SUB
        send_even[at : at + SUB, :] = jnp.where(ty_even, right, left)
        send_odd[at : at + SUB, :] = jnp.where(ty_even, left, right)


class Grid:
    def __init__(self, ref, layers, rows):
        self.layers, self.rows = layers, rows
        self.ring, self.width = ref.shape[1:]
        names = ("cx", "cy", "via", "cx_low", "cy_low", "diagonal", "inverse", "weight")
        at = 0
        for name in names:
            depth = layers - 1 if name == "via" else layers
            setattr(self, name, [ref.at[at + p] for p in range(depth)])
            at += depth
        self.planes = at

    def below(self, v):
        return pltpu.roll(v, self.ring - 1, 0)

    def above(self, v):
        return pltpu.roll(v, 1, 0)

    def right(self, v):
        return pltpu.roll(v, self.width - 1, 1)

    def left(self, v):
        return pltpu.roll(v, 1, 1)

    def couple(self, v, p):
        total = None
        if v[p] is not None:
            total = (
                self.cx[p][...] * self.below(v[p])
                + self.cx_low[p][...] * self.above(v[p])
                + self.cy[p][...] * self.right(v[p])
                + self.cy_low[p][...] * self.left(v[p])
            )
        if p + 1 < self.layers and v[p + 1] is not None:
            term = self.via[p][...] * v[p + 1]
            total = term if total is None else total + term
        if p > 0 and v[p - 1] is not None:
            term = self.via[p - 1][...] * v[p - 1]
            total = term if total is None else total + term
        return total

    def smooth(self, b):
        scaled = [None if v is None else self.inverse[p][...] * v for p, v in enumerate(b)]
        result = []
        for p in range(self.layers):
            total = self.couple(scaled, p)
            if total is not None:
                if b[p] is not None:
                    total = total + b[p]
                total = self.inverse[p][...] * total
            result.append(total)
        return result

    def apply(self, z):
        result = []
        for p in range(self.layers):
            term = self.couple(z, p)
            if z[p] is not None:
                term = self.diagonal[p][...] * z[p] - term
            elif term is not None:
                term = -term
            result.append(term)
        return result

    def flow(self, u):
        result = []
        for p in range(self.layers):
            term = self.cx[p][...] * self.below(u[p]) + self.cy[p][...] * self.right(u[p])
            if p + 1 < self.layers:
                term = term + self.via[p][...] * u[p + 1]
            result.append(self.diagonal[p][...] * u[p] - 2.0 * term)
        return result

    def products(self, b, z, q, u):
        flow = self.flow(u)
        found = []
        for one, two in ((b, z), (z, q), (q, u), (u, flow)):
            total = None
            for left, right in zip(one, two):
                if left is None or right is None:
                    continue
                term = left[0 : self.rows, 0:LANES] * right[0 : self.rows, 0:LANES]
                total = term if total is None else total + term
            found.append(jnp.sum(total, axis=0, keepdims=True))
        return found


def adjoint(layers, shape, refs):
    planes, rims, middle, even, odd, message, grid, base, fields, ground = refs
    rows, ring = shape
    width = 2 * LANES
    tx, ty = lax.axis_index("tx"), lax.axis_index("ty")
    ty_even = lax.rem(ty, 2) == 0
    op = Grid(grid, layers, rows)
    targets = [*op.cx, *op.cy, *op.via, *(ground.at[p] for p in range(layers)), *op.weight]

    slot = lanes_of((SUB, LANES)) // HALO
    tiles = tiles_of((planes, rims, middle))
    for first in range(0, len(tiles), SLOTS):
        q = first // SLOTS * SUB
        one, two = even[q : q + SUB, :], odd[q : q + SUB, :]
        after, before = jnp.where(ty_even, one, two), jnp.where(ty_even, two, one)
        for s, (ref, index) in enumerate(tiles[first : first + SLOTS]):
            both = jnp.where(slot == s, after, before)
            both = pltpu.roll(both, LANES - HALO * s, 1) if s else both
            if ref is middle:
                base[index[0], 0:LANES] = ref[index]
                base[index[0], LANES:] = both
            else:
                at = slice(rows, ring) if ref is rims else index[1]
                targets[index[0]][at, 0:LANES] = ref[index]
                targets[index[0]][at, LANES:] = both

    row, lane = rows_of((ring, width)), lanes_of((ring, width))
    inside = (
        ((row < rows) | (row >= rows + HALO) | (tx < lax.axis_size("tx") - 1))
        & ((row < rows + HALO) | (tx > 0))
        & ((lane < LANES) | (lane >= width - HALO) | ((lane < LANES + HALO) & (ty < lax.axis_size("ty") - 1)))
        & ((lane < width - HALO) | (ty > 0))
    )
    for p in range(layers):
        cx, cy = op.cx[p][...], op.cy[p][...]
        cx_low = jnp.where((row == 0) & (tx == 0), 0.0, op.above(cx))
        cy_low = jnp.where((lane == 0) & (ty == 0), 0.0, op.left(cy))
        total = ground[p] + cx + cx_low + cy + cy_low
        if p + 1 < layers:
            total = total + op.via[p][...]
        if p > 0:
            total = total + op.via[p - 1][...]
        op.cx_low[p][...] = cx_low
        op.cy_low[p][...] = cy_low
        op.diagonal[p][...] = total
        op.inverse[p][...] = jnp.where(inside, 1.0 / total, 0.0)

    z = op.smooth([ref[...] for ref in op.weight])
    q = op.apply(z)
    u = op.smooth(q)
    message[0:rows, :] = z[0][0:rows, 0:LANES]
    message[rows : 2 * rows, :] = u[0][0:rows, 0:LANES]
    for k, field in enumerate((z, q, u)):
        for p in range(layers):
            fields[k * layers + p] = field[p]


def forward(layers, shape, refs):
    grid, base, fields, zed, you, scalars = refs
    rows, ring = shape
    op = Grid(grid, layers, rows)
    b = [base[...]] + [None] * (layers - 1)
    z = op.smooth(b)
    q = op.apply(z)
    u = op.smooth(q)
    for p in range(layers):
        if z[p] is not None:
            zed[p] = z[p][0:rows, 0:LANES]
        you[p] = u[p][0:rows, 0:LANES]
    found = op.products(b, z, q, u)
    z, q, u = ([fields[k * layers + p] for p in range(layers)] for k in range(3))
    found += op.products([ref[...] for ref in op.weight], z, q, u)
    scalars[...] = jnp.concatenate(found, axis=0)


def choose(count, rows, refs):
    chooser = refs[0]
    messages = refs[1 : 1 + count]
    chosen = refs[1 + count]
    hot = chooser[...]
    for half in range(2):
        field = jnp.concatenate([ref[half * rows : (half + 1) * rows, :] for ref in messages], axis=0)
        high, middle, low = three_parts(field)
        chosen[:, half * LANES : (half + 1) * LANES] = dot(hot, high) + dot(hot, middle) + dot(hot, low)


def finish(ways, refs):
    sums = refs[:ways]
    zed, you, chosen, drop, sense = refs[ways:]
    total = sums[0][...]
    for ref in sums[1:]:
        total = total + ref[...]
    total = jnp.broadcast_to(jnp.sum(total, axis=1, keepdims=True), (SUB, LANES))
    for which in range(2):
        bz, zq, qu, uw = (total[4 * which + i : 4 * which + i + 1] for i in range(4))
        ratio = qu / zq
        step = bz / zq
        second = (zq - ratio * bz) / (uw - ratio * qu)
        first = step - second * ratio
        if which == 0:
            for p in range(you.shape[0]):
                part = second * you[p]
                drop[p] = first * zed[p] + part if p < zed.shape[0] else part
        else:
            sense[...] = first * chosen[:, 0:LANES] + second * chosen[:, LANES:]


def vmem():
    return pl.BlockSpec(memory_space=pltpu.VMEM)


def call(kernel, outs, args, scratch=(), specs=None, flops=0, spare=16384):
    size = sum(a.size * a.dtype.itemsize for a in list(args) + list(outs))
    return pl.pallas_call(
        kernel,
        out_shape=tuple(outs),
        in_specs=specs or [vmem() for _ in args],
        out_specs=tuple(vmem() for _ in outs),
        scratch_shapes=scratch,
        cost_estimate=pl.CostEstimate(flops=flops, bytes_accessed=size, transcendentals=0),
        compiler_params=pltpu.CompilerParams(vmem_limit_bytes=(64 * 1024 - spare) * 1024),
    )(*args)


def exchange(values, axis):
    plan = rounds(lax.axis_index(axis), lax.axis_size(axis))
    return [
        lax.ppermute(value, axis, list(enumerate(target)))
        for value, (target, _, _) in zip(values, plan)
    ]


def body(cell_current, block_row, block_count, cond_x, cond_y, cond_via, ground, drop_weight):
    blocks, width = cell_current.shape
    layers, rows, _ = cond_x.shape
    count, ways = lax.axis_size("tx"), lax.axis_size("ty")
    ring = rows + 2 * HALO
    shape = (rows, ring)
    fields = (cond_x, cond_y, cond_via, ground, drop_weight)
    planes = sum(f.shape[0] for f in fields)
    block_row = block_row.reshape(1, blocks)
    hbm = pl.BlockSpec(memory_space=pltpu.HBM)

    def array(*dims, dtype=F32):
        return jax.ShapeDtypeStruct(dims, dtype)

    edges = (planes + 1) // 2 * SUB
    lengths = [ring + (edges if k < 2 else 0) for k in range(count - 1)]
    held, own, home, *sends = call(
        lambda *refs: begin(count, shape, refs),
        [array(planes, rows, LANES), array(ring, LANES), array(1, blocks, dtype=jnp.int32)]
        + [array(n, LANES) for n in lengths],
        (
            *(
                pltpu.with_memory_space_constraint(f, pltpu.HBM)
                for f in (*fields, cell_current, block_row)
            ),
            block_count,
        ),
        scratch=[
            pltpu.VMEM((blocks, LANES), F32),
            pltpu.VMEM((count * ring, blocks), F32),
            pltpu.VMEM((1, blocks), jnp.int32),
            pltpu.SemaphoreType.DMA((len(fields) + 2,)),
        ],
        specs=[hbm] * 7 + [pl.BlockSpec(memory_space=pltpu.SMEM)],
    )
    got = exchange(sends, "tx")
    (chooser,) = call(
        functools.partial(order, count, rows),
        (array(blocks, count * rows, dtype=BF16),),
        (home,),
    )
    packed = array(pl.cdiv(planes * (rows // SUB + 1) + ring // SUB, SLOTS) * SUB, LANES)
    middle, rims, *sends = call(
        lambda *refs: columns(count, shape, refs),
        (array(ring, LANES), array(planes, SUB, LANES), packed, packed),
        (held, own, *in_turn(got, ROW_TURNS)),
    )
    even, odd = exchange(sends, "ty")
    width2 = 2 * LANES
    message, *state = call(
        lambda *refs: adjoint(layers, shape, refs),
        (
            array(2 * rows, LANES),
            array(8 * layers - 1, ring, width2),
            array(ring, width2),
            array(3 * layers, ring, width2),
        ),
        (held, rims, middle, even, odd),
        scratch=[pltpu.VMEM((layers, ring, width2), F32)],
    )
    messages = in_turn(exchange([message] * (count - 1), "tx"), DATA_TURNS) + [message]
    zed, you, total = call(
        lambda *refs: forward(layers, shape, refs),
        (array(min(2, layers), rows, LANES), array(layers, rows, LANES), array(SUB, LANES)),
        state,
    )
    total = functools.reduce(jnp.add, [total] + exchange([total] * (count - 1), "tx"))
    totals = [total] + exchange([total] * (ways - 1), "ty")
    (chosen,) = call(
        lambda *refs: choose(count, rows, refs),
        (array(blocks, 2 * LANES),),
        (chooser, *messages),
    )
    return call(
        lambda *refs: finish(ways, refs),
        (array(layers, rows, LANES), array(blocks, width)),
        (*totals, zed, you, chosen),
    )


def solution(mesh):
    placed = (
        P(("grp", "tx"), "ty"),
        P(("grp", "tx")),
        P(("grp", "tx")),
        P(None, ("grp", "tx"), "ty"),
        P(None, ("grp", "tx"), "ty"),
        P(None, ("grp", "tx"), "ty"),
        P(None, ("grp", "tx"), "ty"),
        P(None, ("grp", "tx"), "ty"),
    )
    return jax.shard_map(
        body,
        mesh=mesh,
        in_specs=placed,
        out_specs=(P(None, ("grp", "tx"), "ty"), P(("grp", "tx"), "ty")),
        check_vma=False,
    )
```

```python
import functools

import jax
import jax.numpy as jnp
from jax import lax
from jax.experimental import pallas as pl
from jax.experimental.pallas import tpu as pltpu
from jax.sharding import PartitionSpec as P

HALO = 4
SUB = 8
LANES = 128
SLOTS = LANES // HALO
F32 = jnp.float32
BF16 = jnp.bfloat16
ROW_TURNS = (1, 0, 2)
DATA_TURNS = (1, 0, 2)


def lanes_of(shape):
    return lax.broadcasted_iota(jnp.int32, shape, len(shape) - 1)


def rows_of(shape):
    return lax.broadcasted_iota(jnp.int32, shape, len(shape) - 2)


def tiles_of(refs):
    found = []
    for ref in refs:
        rows = ref.shape[-2]
        for plane in range(ref.shape[0] if len(ref.shape) == 3 else 1):
            for at in range(0, rows, SUB):
                if len(ref.shape) == 3:
                    found.append((ref, (plane, slice(at, at + SUB), slice(None))))
                else:
                    found.append((ref, (slice(at, at + SUB), slice(None))))
    return found


def three_parts(value):
    high = value.astype(BF16)
    rest = value - high.astype(F32)
    middle = rest.astype(BF16)
    low = (rest - middle.astype(F32)).astype(BF16)
    return high, middle, low


def dot(left, right):
    return jnp.dot(left, right, preferred_element_type=F32)


def in_turn(values, turns, back=False):
    turns = turns + tuple(range(len(turns), len(values)))
    if back:
        turns = tuple(turns.index(k) for k in range(len(values)))
    return [values[k] for k in turns]


def rounds(index, count):
    even = [(i + 1) % count if i % 2 == 0 else (i - 1) % count for i in range(count)]
    odd = [(i - 1) % count if i % 2 == 0 else (i + 1) % count for i in range(count)]
    is_even = lax.rem(index, 2) == 0
    up, down = lax.rem(index + 1, count), lax.rem(index + count - 1, count)
    plan = [
        (even, jnp.where(is_even, up, down), jnp.where(is_even, up, down)),
        (odd, jnp.where(is_even, down, up), jnp.where(is_even, down, up)),
    ]
    for k in range(2, count - 1):
        target = [(i + k) % count for i in range(count)]
        plan.append((target, lax.rem(index + k, count), lax.rem(index - k + count, count)))
    return plan


def begin(count, shape, refs):
    fields, cell_in, row_in, block_count = refs[:5], refs[5], refs[6], refs[7]
    planes, own, home = refs[8:11]
    sends = refs[11 : 11 + count - 1]
    cell, picker, block_row, sems = refs[11 + count - 1 :]
    rows, ring = shape
    fetch_row = pltpu.make_async_copy(row_in, block_row, sems.at[6])
    fetch_row.start()
    fetch_cell = pltpu.make_async_copy(cell_in, cell, sems.at[0])
    fetch_cell.start()
    fetches, at = [], 0
    for i, ref in enumerate(fields):
        part = planes.at[at : at + ref.shape[0]]
        fetches.append(pltpu.make_async_copy(ref, part, sems.at[i + 1]))
        fetches[-1].start()
        at += ref.shape[0]

    me = lax.axis_index("tx")
    even = lax.rem(me, 2) == 0
    blocks = block_row.shape[1]
    line = rows_of((ring, blocks))
    line = jnp.where(line < rows + HALO, line, line - ring)
    fetch_row.wait()
    live = lanes_of((1, blocks)) < block_count[0]
    land = jnp.where(live, block_row[...], -rows)
    home[...] = land
    targets = [me] + [target for _, target, _ in rounds(me, count)]
    for k, target in enumerate(targets):
        picker[k * ring : (k + 1) * ring, :] = (line == land - target * rows).astype(F32)
    hot = picker[...].astype(BF16)
    fetch_cell.wait()
    high, middle, low = three_parts(cell[...])
    sums = dot(hot, high) + dot(hot, middle) + dot(hot, low)
    own[...] = sums[0:ring]
    for k, send in enumerate(sends):
        send[0:ring, :] = sums[(k + 1) * ring : (k + 2) * ring]

    for fetch in fetches:
        fetch.wait()
    lower = rows_of((SUB, LANES)) < HALO
    for p in range(0, planes.shape[0], 2):
        first = planes[p, 0:SUB, :]
        last = planes[p, rows - SUB : rows, :]
        if p + 1 < planes.shape[0]:
            first = jnp.where(lower, first, pltpu.roll(planes[p + 1, 0:SUB, :], HALO, 0))
            last = jnp.where(lower, pltpu.roll(planes[p + 1, rows - SUB : rows, :], HALO, 0), last)
        at = ring + p // 2 * SUB
        sends[0][at : at + SUB, :] = jnp.where(even, last, first)
        sends[1][at : at + SUB, :] = jnp.where(even, first, last)


def order(count, rows, home, chooser):
    me = lax.axis_index("tx")
    blocks = home.shape[1]
    line = rows_of((rows, blocks))
    for k, source in enumerate(in_turn([source for _, _, source in rounds(me, count)], DATA_TURNS) + [me]):
        hot = (line == home[...] - source * rows).astype(F32)
        chooser[:, k * rows : (k + 1) * rows] = hot.T.astype(BF16)


def columns(count, shape, refs):
    planes, own = refs[:2]
    got = in_turn(refs[2 : 2 + count - 1], ROW_TURNS, True)
    base, rims, send_even, send_odd = refs[2 + count - 1 :]
    rows, ring = shape
    tx_even = lax.rem(lax.axis_index("tx"), 2) == 0
    ty_even = lax.rem(lax.axis_index("ty"), 2) == 0
    lower = rows_of((SUB, LANES)) < HALO
    for i in range(0, ring, SUB):
        total = own[i : i + SUB, :]
        for ref in got:
            total = total + ref[i : i + SUB, :]
        base[i : i + SUB, :] = total
    for p in range(0, planes.shape[0], 2):
        at = ring + p // 2 * SUB
        one, two = got[0][at : at + SUB, :], got[1][at : at + SUB, :]
        after = jnp.where(tx_even, one, two)
        before = jnp.where(tx_even, two, one)
        rims[p] = jnp.where(lower, after, before)
        if p + 1 < planes.shape[0]:
            rims[p + 1] = pltpu.roll(jnp.where(lower, before, after), HALO, 0)

    slot = lanes_of((SUB, LANES)) // HALO
    tiles = tiles_of((planes, rims, base))
    for first in range(0, len(tiles), SLOTS):
        left = jnp.zeros((SUB, LANES), F32)
        right = left
        for s, (ref, index) in enumerate(tiles[first : first + SLOTS]):
            turned = pltpu.roll(ref[index], HALO * s, 1) if s else ref[index]
            left = jnp.where(slot == s, turned, left)
            right = jnp.where(slot == (s - 1) % SLOTS, turned, right)
        at = first // SLOTS * SUB
        send_even[at : at + SUB, :] = jnp.where(ty_even, right, left)
        send_odd[at : at + SUB, :] = jnp.where(ty_even, left, right)


class Grid:
    def __init__(self, ref, layers, rows):
        self.layers, self.rows = layers, rows
        self.ring, self.width = ref.shape[1:]
        names = ("cx", "cy", "via", "cx_low", "cy_low", "diagonal", "inverse", "weight")
        at = 0
        for name in names:
            depth = layers - 1 if name == "via" else layers
            setattr(self, name, [ref.at[at + p] for p in range(depth)])
            at += depth
        self.planes = at

    def below(self, v):
        return pltpu.roll(v, self.ring - 1, 0)

    def above(self, v):
        return pltpu.roll(v, 1, 0)

    def right(self, v):
        return pltpu.roll(v, self.width - 1, 1)

    def left(self, v):
        return pltpu.roll(v, 1, 1)

    def couple(self, v, p):
        total = None
        if v[p] is not None:
            total = (
                self.cx[p][...] * self.below(v[p])
                + self.cx_low[p][...] * self.above(v[p])
                + self.cy[p][...] * self.right(v[p])
                + self.cy_low[p][...] * self.left(v[p])
            )
        if p + 1 < self.layers and v[p + 1] is not None:
            term = self.via[p][...] * v[p + 1]
            total = term if total is None else total + term
        if p > 0 and v[p - 1] is not None:
            term = self.via[p - 1][...] * v[p - 1]
            total = term if total is None else total + term
        return total

    def smooth(self, b):
        scaled = [None if v is None else self.inverse[p][...] * v for p, v in enumerate(b)]
        result = []
        for p in range(self.layers):
            total = self.couple(scaled, p)
            if total is not None:
                if b[p] is not None:
                    total = total + b[p]
                total = self.inverse[p][...] * total
            result.append(total)
        return result

    def apply(self, z):
        result = []
        for p in range(self.layers):
            term = self.couple(z, p)
            if z[p] is not None:
                term = self.diagonal[p][...] * z[p] - term
            elif term is not None:
                term = -term
            result.append(term)
        return result

    def flow(self, u):
        result = []
        for p in range(self.layers):
            term = self.cx[p][...] * self.below(u[p]) + self.cy[p][...] * self.right(u[p])
            if p + 1 < self.layers:
                term = term + self.via[p][...] * u[p + 1]
            result.append(self.diagonal[p][...] * u[p] - 2.0 * term)
        return result

    def products(self, b, z, q, u):
        flow = self.flow(u)
        found = []
        for one, two in ((b, z), (z, q), (q, u), (u, flow)):
            total = None
            for left, right in zip(one, two):
                if left is None or right is None:
                    continue
                term = left[0 : self.rows, 0:LANES] * right[0 : self.rows, 0:LANES]
                total = term if total is None else total + term
            found.append(jnp.sum(total, axis=0, keepdims=True))
        return found


def solve(layers, shape, refs):
    planes, rims, middle, even, odd, message, zed, you, scalars, grid, base, ground = refs
    rows, ring = shape
    width = 2 * LANES
    tx, ty = lax.axis_index("tx"), lax.axis_index("ty")
    ty_even = lax.rem(ty, 2) == 0
    op = Grid(grid, layers, rows)
    targets = [*op.cx, *op.cy, *op.via, *(ground.at[p] for p in range(layers)), *op.weight]

    slot = lanes_of((SUB, LANES)) // HALO
    tiles = tiles_of((planes, rims, middle))
    for first in range(0, len(tiles), SLOTS):
        q = first // SLOTS * SUB
        one, two = even[q : q + SUB, :], odd[q : q + SUB, :]
        after, before = jnp.where(ty_even, one, two), jnp.where(ty_even, two, one)
        for s, (ref, index) in enumerate(tiles[first : first + SLOTS]):
            both = jnp.where(slot == s, after, before)
            both = pltpu.roll(both, LANES - HALO * s, 1) if s else both
            if ref is middle:
                base[index[0], 0:LANES] = ref[index]
                base[index[0], LANES:] = both
            else:
                at = slice(rows, ring) if ref is rims else index[1]
                targets[index[0]][at, 0:LANES] = ref[index]
                targets[index[0]][at, LANES:] = both

    row, lane = rows_of((ring, width)), lanes_of((ring, width))
    inside = (
        ((row < rows) | (row >= rows + HALO) | (tx < lax.axis_size("tx") - 1))
        & ((row < rows + HALO) | (tx > 0))
        & ((lane < LANES) | (lane >= width - HALO) | ((lane < LANES + HALO) & (ty < lax.axis_size("ty") - 1)))
        & ((lane < width - HALO) | (ty > 0))
    )
    for p in range(layers):
        cx, cy = op.cx[p][...], op.cy[p][...]
        cx_low = jnp.where((row == 0) & (tx == 0), 0.0, op.above(cx))
        cy_low = jnp.where((lane == 0) & (ty == 0), 0.0, op.left(cy))
        total = ground[p] + cx + cx_low + cy + cy_low
        if p + 1 < layers:
            total = total + op.via[p][...]
        if p > 0:
            total = total + op.via[p - 1][...]
        op.cx_low[p][...] = cx_low
        op.cy_low[p][...] = cy_low
        op.diagonal[p][...] = total
        op.inverse[p][...] = jnp.where(inside, 1.0 / total, 0.0)

    z = op.smooth([ref[...] for ref in op.weight])
    q = op.apply(z)
    u = op.smooth(q)
    message[0:rows, :] = z[0][0:rows, 0:LANES]
    message[rows : 2 * rows, :] = u[0][0:rows, 0:LANES]
    b = [base[...]] + [None] * (layers - 1)
    found = op.products([ref[...] for ref in op.weight], z, q, u)
    z = op.smooth(b)
    q = op.apply(z)
    u = op.smooth(q)
    for p in range(layers):
        if z[p] is not None:
            zed[p] = z[p][0:rows, 0:LANES]
        you[p] = u[p][0:rows, 0:LANES]
    found = jnp.concatenate(op.products(b, z, q, u) + found, axis=0)
    scalars[...] = found
    message[2 * rows :, :] = found


def choose(count, rows, refs):
    chooser = refs[0]
    messages = refs[1 : 1 + count]
    chosen = refs[1 + count]
    hot = chooser[...]
    for half in range(2):
        field = jnp.concatenate([ref[half * rows : (half + 1) * rows, :] for ref in messages], axis=0)
        high, middle, low = three_parts(field)
        chosen[:, half * LANES : (half + 1) * LANES] = dot(hot, high) + dot(hot, middle) + dot(hot, low)


def finish(ways, refs):
    sums = refs[:ways]
    zed, you, chosen, drop, sense = refs[ways:]
    total = sums[0][...]
    for ref in sums[1:]:
        total = total + ref[...]
    total = jnp.broadcast_to(jnp.sum(total, axis=1, keepdims=True), (SUB, LANES))
    for which in range(2):
        bz, zq, qu, uw = (total[4 * which + i : 4 * which + i + 1] for i in range(4))
        ratio = qu / zq
        step = bz / zq
        left = uw - ratio * qu
        second = jnp.where(left > 2e-7 * uw, (zq - ratio * bz) / left, -step)
        first = step - second * ratio
        if which == 0:
            for p in range(you.shape[0]):
                part = second * you[p]
                drop[p] = first * zed[p] + part if p < zed.shape[0] else part
        else:
            sense[...] = first * chosen[:, 0:LANES] + second * chosen[:, LANES:]


def vmem():
    return pl.BlockSpec(memory_space=pltpu.VMEM)


def call(kernel, outs, args, scratch=(), specs=None, flops=0, spare=16384):
    size = sum(a.size * a.dtype.itemsize for a in list(args) + list(outs))
    return pl.pallas_call(
        kernel,
        out_shape=tuple(outs),
        in_specs=specs or [vmem() for _ in args],
        out_specs=tuple(vmem() for _ in outs),
        scratch_shapes=scratch,
        cost_estimate=pl.CostEstimate(flops=flops, bytes_accessed=size, transcendentals=0),
        compiler_params=pltpu.CompilerParams(vmem_limit_bytes=(64 * 1024 - spare) * 1024),
    )(*args)


def exchange(values, axis):
    plan = rounds(lax.axis_index(axis), lax.axis_size(axis))
    return [
        lax.ppermute(value, axis, list(enumerate(target)))
        for value, (target, _, _) in zip(values, plan)
    ]


def body(cell_current, block_row, block_count, cond_x, cond_y, cond_via, ground, drop_weight):
    blocks, width = cell_current.shape
    layers, rows, _ = cond_x.shape
    count, ways = lax.axis_size("tx"), lax.axis_size("ty")
    ring = rows + 2 * HALO
    shape = (rows, ring)
    fields = (cond_x, cond_y, cond_via, ground, drop_weight)
    planes = sum(f.shape[0] for f in fields)
    block_row = block_row.reshape(1, blocks)
    hbm = pl.BlockSpec(memory_space=pltpu.HBM)

    def array(*dims, dtype=F32):
        return jax.ShapeDtypeStruct(dims, dtype)

    edges = (planes + 1) // 2 * SUB
    lengths = [ring + (edges if k < 2 else 0) for k in range(count - 1)]
    held, own, home, *sends = call(
        lambda *refs: begin(count, shape, refs),
        [array(planes, rows, LANES), array(ring, LANES), array(1, blocks, dtype=jnp.int32)]
        + [array(n, LANES) for n in lengths],
        (
            *(
                pltpu.with_memory_space_constraint(f, pltpu.HBM)
                for f in (*fields, cell_current, block_row)
            ),
            block_count,
        ),
        scratch=[
            pltpu.VMEM((blocks, LANES), F32),
            pltpu.VMEM((count * ring, blocks), F32),
            pltpu.VMEM((1, blocks), jnp.int32),
            pltpu.SemaphoreType.DMA((len(fields) + 2,)),
        ],
        specs=[hbm] * 7 + [pl.BlockSpec(memory_space=pltpu.SMEM)],
    )
    got = exchange(sends, "tx")
    (chooser,) = call(
        functools.partial(order, count, rows),
        (array(blocks, count * rows, dtype=BF16),),
        (home,),
    )
    packed = array(pl.cdiv(planes * (rows // SUB + 1) + ring // SUB, SLOTS) * SUB, LANES)
    middle, rims, *sends = call(
        lambda *refs: columns(count, shape, refs),
        (array(ring, LANES), array(planes, SUB, LANES), packed, packed),
        (held, own, *in_turn(got, ROW_TURNS)),
    )
    even, odd = exchange(sends, "ty")
    width2 = 2 * LANES
    message, zed, you, total = call(
        lambda *refs: solve(layers, shape, refs),
        (
            array(2 * rows + SUB, LANES),
            array(min(2, layers), rows, LANES),
            array(layers, rows, LANES),
            array(SUB, LANES),
        ),
        (held, rims, middle, even, odd),
        scratch=[
            pltpu.VMEM((8 * layers - 1, ring, width2), F32),
            pltpu.VMEM((ring, width2), F32),
            pltpu.VMEM((layers, ring, width2), F32),
        ],
    )
    got = exchange([message] * (count - 1), "tx")
    ahead = exchange([total] * (count - 1), "tx")[2:]
    total = functools.reduce(jnp.add, [total] + [m[2 * rows :] for m in got[:2]] + ahead)
    messages = in_turn(got, DATA_TURNS) + [message]
    totals = [total] + exchange([total] * (ways - 1), "ty")
    (chosen,) = call(
        lambda *refs: choose(count, rows, refs),
        (array(blocks, 2 * LANES),),
        (chooser, *messages),
    )
    return call(
        lambda *refs: finish(ways, refs),
        (array(layers, rows, LANES), array(blocks, width)),
        (*totals, zed, you, chosen),
    )


def solution(mesh):
    placed = (
        P(("grp", "tx"), "ty"),
        P(("grp", "tx")),
        P(("grp", "tx")),
        P(None, ("grp", "tx"), "ty"),
        P(None, ("grp", "tx"), "ty"),
        P(None, ("grp", "tx"), "ty"),
        P(None, ("grp", "tx"), "ty"),
        P(None, ("grp", "tx"), "ty"),
    )
    return jax.shard_map(
        body,
        mesh=mesh,
        in_specs=placed,
        out_specs=(P(None, ("grp", "tx"), "ty"), P(("grp", "tx"), "ty")),
        check_vma=False,
    )
```

```python
import functools

import jax
import jax.numpy as jnp
from jax import lax
from jax.experimental import pallas as pl
from jax.experimental.pallas import tpu as pltpu
from jax.sharding import PartitionSpec as P

HALO = 4
SUB = 8
LANES = 128
SLOTS = LANES // HALO
WINDOW = 8 * HALO
F32 = jnp.float32
BF16 = jnp.bfloat16
ROW_TURNS = (1, 0, 2)
DATA_TURNS = (1, 0, 2)


def lanes_of(shape):
    return lax.broadcasted_iota(jnp.int32, shape, len(shape) - 1)


def rows_of(shape):
    return lax.broadcasted_iota(jnp.int32, shape, len(shape) - 2)


def tiles_of(refs):
    found = []
    for ref in refs:
        rows = ref.shape[-2]
        for plane in range(ref.shape[0] if len(ref.shape) == 3 else 1):
            for at in range(0, rows, SUB):
                if len(ref.shape) == 3:
                    found.append((ref, (plane, slice(at, at + SUB), slice(None))))
                else:
                    found.append((ref, (slice(at, at + SUB), slice(None))))
    return found


def three_parts(value):
    high = value.astype(BF16)
    rest = value - high.astype(F32)
    middle = rest.astype(BF16)
    low = (rest - middle.astype(F32)).astype(BF16)
    return high, middle, low


def dot(left, right):
    return jnp.dot(left, right, preferred_element_type=F32)


def in_turn(values, turns, back=False):
    turns = turns + tuple(range(len(turns), len(values)))
    if back:
        turns = tuple(turns.index(k) for k in range(len(values)))
    return [values[k] for k in turns]


def rounds(index, count):
    even = [(i + 1) % count if i % 2 == 0 else (i - 1) % count for i in range(count)]
    odd = [(i - 1) % count if i % 2 == 0 else (i + 1) % count for i in range(count)]
    is_even = lax.rem(index, 2) == 0
    up, down = lax.rem(index + 1, count), lax.rem(index + count - 1, count)
    plan = [
        (even, jnp.where(is_even, up, down), jnp.where(is_even, up, down)),
        (odd, jnp.where(is_even, down, up), jnp.where(is_even, down, up)),
    ]
    for k in range(2, count - 1):
        target = [(i + k) % count for i in range(count)]
        plan.append((target, lax.rem(index + k, count), lax.rem(index - k + count, count)))
    return plan


def begin(count, shape, refs):
    fields, cell_in, row_in, block_count = refs[:5], refs[5], refs[6], refs[7]
    planes, own, home = refs[8:11]
    sends = refs[11 : 11 + count - 1]
    cell, picker, block_row, sems = refs[11 + count - 1 :]
    rows, ring = shape
    fetch_row = pltpu.make_async_copy(row_in, block_row, sems.at[6])
    fetch_row.start()
    fetch_cell = pltpu.make_async_copy(cell_in, cell, sems.at[0])
    fetch_cell.start()
    fetches, at = [], 0
    for i, ref in enumerate(fields):
        part = planes.at[at : at + ref.shape[0]]
        fetches.append(pltpu.make_async_copy(ref, part, sems.at[i + 1]))
        fetches[-1].start()
        at += ref.shape[0]

    me = lax.axis_index("tx")
    even = lax.rem(me, 2) == 0
    blocks = block_row.shape[1]
    line = rows_of((ring, blocks))
    line = jnp.where(line < rows + HALO, line, line - ring)
    fetch_row.wait()
    live = lanes_of((1, blocks)) < block_count[0]
    land = jnp.where(live, block_row[...], -rows)
    home[...] = land
    targets = [me] + [target for _, target, _ in rounds(me, count)]
    for k, target in enumerate(targets):
        picker[k * ring : (k + 1) * ring, :] = (line == land - target * rows).astype(F32)
    hot = picker[...].astype(BF16)
    fetch_cell.wait()
    high, middle, low = three_parts(cell[...])
    sums = dot(hot, high) + dot(hot, middle) + dot(hot, low)
    own[...] = sums[0:ring]
    for k, send in enumerate(sends):
        send[0:ring, :] = sums[(k + 1) * ring : (k + 2) * ring]

    for fetch in fetches:
        fetch.wait()
    lower = rows_of((SUB, LANES)) < HALO
    for p in range(0, planes.shape[0], 2):
        first = planes[p, 0:SUB, :]
        last = planes[p, rows - SUB : rows, :]
        if p + 1 < planes.shape[0]:
            first = jnp.where(lower, first, pltpu.roll(planes[p + 1, 0:SUB, :], HALO, 0))
            last = jnp.where(lower, pltpu.roll(planes[p + 1, rows - SUB : rows, :], HALO, 0), last)
        at = ring + p // 2 * SUB
        sends[0][at : at + SUB, :] = jnp.where(even, last, first)
        sends[1][at : at + SUB, :] = jnp.where(even, first, last)


def order(count, rows, home, chooser):
    me = lax.axis_index("tx")
    blocks = home.shape[1]
    line = rows_of((rows, blocks))
    for k, source in enumerate(in_turn([source for _, _, source in rounds(me, count)], DATA_TURNS) + [me]):
        hot = (line == home[...] - source * rows).astype(F32)
        chooser[:, k * rows : (k + 1) * rows] = hot.T.astype(BF16)


def columns(count, shape, refs):
    planes, own = refs[:2]
    got = in_turn(refs[2 : 2 + count - 1], ROW_TURNS, True)
    base, rims, send_even, send_odd = refs[2 + count - 1 :]
    rows, ring = shape
    tx_even = lax.rem(lax.axis_index("tx"), 2) == 0
    ty_even = lax.rem(lax.axis_index("ty"), 2) == 0
    lower = rows_of((SUB, LANES)) < HALO
    for i in range(0, ring, SUB):
        total = own[i : i + SUB, :]
        for ref in got:
            total = total + ref[i : i + SUB, :]
        base[i : i + SUB, :] = total
    for p in range(0, planes.shape[0], 2):
        at = ring + p // 2 * SUB
        one, two = got[0][at : at + SUB, :], got[1][at : at + SUB, :]
        after = jnp.where(tx_even, one, two)
        before = jnp.where(tx_even, two, one)
        rims[p] = jnp.where(lower, after, before)
        if p + 1 < planes.shape[0]:
            rims[p + 1] = pltpu.roll(jnp.where(lower, before, after), HALO, 0)

    slot = lanes_of((SUB, LANES)) // HALO
    tiles = tiles_of((planes, rims, base))
    for first in range(0, len(tiles), SLOTS):
        left = jnp.zeros((SUB, LANES), F32)
        right = left
        for s, (ref, index) in enumerate(tiles[first : first + SLOTS]):
            turned = pltpu.roll(ref[index], HALO * s, 1) if s else ref[index]
            left = jnp.where(slot == s, turned, left)
            right = jnp.where(slot == (s - 1) % SLOTS, turned, right)
        at = first // SLOTS * SUB
        send_even[at : at + SUB, :] = jnp.where(ty_even, right, left)
        send_odd[at : at + SUB, :] = jnp.where(ty_even, left, right)


class Grid:
    def __init__(self, ref, layers, rows):
        self.layers, self.rows = layers, rows
        self.ring, self.width = ref.shape[1:]
        names = ("cx", "cy", "via", "cx_low", "cy_low", "diagonal", "inverse", "weight")
        at = 0
        for name in names:
            depth = layers - 1 if name == "via" else layers
            setattr(self, name, [ref.at[at + p] for p in range(depth)])
            at += depth
        self.planes = at

    def below(self, v):
        return pltpu.roll(v, self.ring - 1, 0)

    def above(self, v):
        return pltpu.roll(v, 1, 0)

    def right(self, v):
        return pltpu.roll(v, self.width - 1, 1)

    def left(self, v):
        return pltpu.roll(v, 1, 1)

    def couple(self, v, p):
        total = None
        if v[p] is not None:
            total = (
                self.cx[p][...] * self.below(v[p])
                + self.cx_low[p][...] * self.above(v[p])
                + self.cy[p][...] * self.right(v[p])
                + self.cy_low[p][...] * self.left(v[p])
            )
        if p + 1 < self.layers and v[p + 1] is not None:
            term = self.via[p][...] * v[p + 1]
            total = term if total is None else total + term
        if p > 0 and v[p - 1] is not None:
            term = self.via[p - 1][...] * v[p - 1]
            total = term if total is None else total + term
        return total

    def smooth(self, b):
        scaled = [None if v is None else self.inverse[p][...] * v for p, v in enumerate(b)]
        result = []
        for p in range(self.layers):
            total = self.couple(scaled, p)
            if total is not None:
                if b[p] is not None:
                    total = total + b[p]
                total = self.inverse[p][...] * total
            result.append(total)
        return result

    def apply(self, z):
        result = []
        for p in range(self.layers):
            term = self.couple(z, p)
            if z[p] is not None:
                term = self.diagonal[p][...] * z[p] - term
            elif term is not None:
                term = -term
            result.append(term)
        return result

    def flow(self, u):
        result = []
        for p in range(self.layers):
            term = self.cx[p][...] * self.below(u[p]) + self.cy[p][...] * self.right(u[p])
            if p + 1 < self.layers:
                term = term + self.via[p][...] * u[p + 1]
            result.append(self.diagonal[p][...] * u[p] - 2.0 * term)
        return result

    def products(self, b, z, q, u, kept):
        flow = self.flow(u)
        found = []
        for one, two in ((b, z), (z, q), (q, u), (u, flow)):
            total = None
            for left, right in zip(one, two):
                if left is None or right is None:
                    continue
                term = left[0 : self.rows, 0:LANES] * right[0 : self.rows, 0:LANES]
                total = term if total is None else total + term
            found.append(jnp.sum(jnp.where(kept, total, 0.0), axis=0, keepdims=True))
        return found


def inner(layers, shape, refs):
    planes, rims, middle, front, zed, you, sums, strips, grid, ground = refs
    rows, ring = shape
    tx = lax.axis_index("tx")
    op = Grid(grid, layers, rows)
    targets = [*op.cx, *op.cy, *op.via, *(ground.at[p] for p in range(layers)), *op.weight]
    for p, target in enumerate(targets):
        target[0:rows, :] = planes[p]
        target[rows:ring, :] = rims[p]

    row = rows_of((ring, LANES))
    inside = ((row < rows) | (row >= rows + HALO) | (tx < lax.axis_size("tx") - 1)) & (
        (row < rows + HALO) | (tx > 0)
    )
    for p in range(layers):
        cx, cy = op.cx[p][...], op.cy[p][...]
        cx_low = jnp.where((row == 0) & (tx == 0), 0.0, op.above(cx))
        cy_low = op.left(cy)
        total = ground[p] + cx + cx_low + cy + cy_low
        if p + 1 < layers:
            total = total + op.via[p][...]
        if p > 0:
            total = total + op.via[p - 1][...]
        op.cx_low[p][...] = cx_low
        op.cy_low[p][...] = cy_low
        op.diagonal[p][...] = total
        op.inverse[p][...] = jnp.where(inside, 1.0 / total, 0.0)

    lane = lanes_of((rows, LANES))
    kept = (lane >= HALO) & (lane < LANES - HALO)
    b = [ref[...] for ref in op.weight]
    z = op.smooth(b)
    q = op.apply(z)
    u = op.smooth(q)
    front[0] = z[0][0:rows]
    front[1] = u[0][0:rows]
    found = op.products(b, z, q, u, kept)
    b = [middle[...]] + [None] * (layers - 1)
    z = op.smooth(b)
    q = op.apply(z)
    u = op.smooth(q)
    for p in range(layers):
        if z[p] is not None:
            zed[p] = z[p][0:rows]
        you[p] = u[p][0:rows]
    sums[...] = jnp.concatenate(op.products(b, z, q, u, kept) + found, axis=0)

    lane = lanes_of((ring, LANES))
    grounds = [ground.at[p] for p in range(layers)]
    for kind, refs_ in enumerate((op.cx, op.cy, op.via, grounds, op.weight, [middle])):
        packed = jnp.zeros((ring, LANES), F32)
        for p, ref in enumerate(refs_):
            at = p * WINDOW
            first = pltpu.roll(ref[...], at + HALO, 1)
            last = pltpu.roll(ref[...], (at + WINDOW - HALO) % LANES, 1)
            packed = jnp.where((lane >= at + HALO) & (lane < at + WINDOW // 2), first, packed)
            packed = jnp.where((lane >= at + WINDOW // 2) & (lane < at + WINDOW - HALO), last, packed)
        strips[kind] = packed


def outer(layers, shape, refs):
    strips, even, odd, front, zed_in, you_in, sums, message, zed, you, scalars, held = refs
    rows, ring = shape
    tx, ty = lax.axis_index("tx"), lax.axis_index("ty")
    ty_even = lax.rem(ty, 2) == 0

    depths = (layers, layers, layers - 1, layers, layers)
    homes = [(kind, p) for kind, depth in enumerate(depths) for p in range(depth)]
    tiles = [(kind, p, at) for kind, p in homes for at in range(0, rows, SUB)]
    tiles += [(kind, p, at) for kind, p in homes for at in range(rows, ring, SUB)]
    tiles += [(len(depths), 0, at) for at in range(0, ring, SUB)]
    parts = {}
    lane = lanes_of((SUB, LANES))
    for j, (kind, p, at) in enumerate(tiles):
        q, s = divmod(j, SLOTS)
        one, two = even[q * SUB : (q + 1) * SUB, :], odd[q * SUB : (q + 1) * SUB, :]
        after, before = jnp.where(ty_even, one, two), jnp.where(ty_even, two, one)
        start = p * WINDOW
        part = parts[kind, at] if (kind, at) in parts else strips[kind, at : at + SUB, :]
        before = pltpu.roll(before, (start + HALO - HALO * s) % LANES, 1)
        after = pltpu.roll(after, (start + WINDOW - HALO - HALO * s) % LANES, 1)
        part = jnp.where((lane >= start) & (lane < start + HALO), before, part)
        part = jnp.where((lane >= start + WINDOW - HALO) & (lane < start + WINDOW), after, part)
        parts[kind, at] = part
    for (kind, at), part in parts.items():
        held[kind, at : at + SUB, :] = part
    cx, cy, via, ground, weight, source = (held[kind] for kind in range(len(depths) + 1))

    def below(v):
        return pltpu.roll(v, ring - 1, 0)

    def right(v):
        return pltpu.roll(v, LANES - 1, 1)

    def upper(v):
        return pltpu.roll(v, LANES - WINDOW, 1)

    row, lane = rows_of((ring, LANES)), lax.rem(lanes_of((ring, LANES)), WINDOW)
    inside = (
        ((row < rows) | (row >= rows + HALO) | (tx < lax.axis_size("tx") - 1))
        & ((row < rows + HALO) | (tx > 0))
        & ((lane < WINDOW - HALO) | (ty < lax.axis_size("ty") - 1))
        & ((lane >= HALO) | (ty > 0))
    )
    cx_low = jnp.where((row == 0) & (tx == 0), 0.0, pltpu.roll(cx, 1, 0))
    cy_low = jnp.where((lane == HALO) & (ty == 0), 0.0, pltpu.roll(cy, 1, 1))
    via_low = pltpu.roll(via, WINDOW, 1)
    diagonal = ground + cx + cx_low + cy + cy_low + via + via_low
    inverse = jnp.where(inside, 1.0 / diagonal, 0.0)

    def couple(v):
        return (
            cx * below(v)
            + cx_low * pltpu.roll(v, 1, 0)
            + cy * right(v)
            + cy_low * pltpu.roll(v, 1, 1)
            + via * upper(v)
            + via_low * pltpu.roll(v, WINDOW, 1)
        )

    def smooth(b):
        return inverse * (b + couple(inverse * b))

    near = lane[0:rows]
    near = ((near >= HALO) & (near < 2 * HALO)) | (
        (near >= WINDOW - 2 * HALO) & (near < WINDOW - HALO)
    )
    column = lanes_of((rows, LANES))

    def whole(middle_part, side, p):
        first = pltpu.roll(side[0:rows], (LANES - HALO - p * WINDOW) % LANES, 1)
        last = pltpu.roll(side[0:rows], (LANES + HALO - (p + 1) * WINDOW) % LANES, 1)
        return jnp.where(
            column < HALO, first, jnp.where(column >= LANES - HALO, last, middle_part)
        )

    found = []
    for which, b in enumerate((source, weight)):
        z = smooth(b)
        q = diagonal * z - couple(z)
        u = smooth(q)
        flow = diagonal * u - 2.0 * (cx * below(u) + cy * right(u) + via * upper(u))
        for one, two in ((b, z), (z, q), (q, u), (u, flow)):
            term = jnp.where(near, one[0:rows] * two[0:rows], 0.0)
            found.append(jnp.sum(term, axis=0, keepdims=True))
        if which == 0:
            for p in range(layers):
                if p < zed.shape[0]:
                    zed[p] = whole(zed_in[p], z, p)
                you[p] = whole(you_in[p], u, p)
        else:
            message[0:rows, :] = whole(front[0], z, 0)
            message[rows : 2 * rows, :] = whole(front[1], u, 0)
    found = sums[...] + jnp.concatenate(found, axis=0)
    scalars[...] = found
    message[2 * rows :, :] = found


def choose(count, rows, refs):
    chooser = refs[0]
    messages = refs[1 : 1 + count]
    chosen = refs[1 + count]
    hot = chooser[...]
    for half in range(2):
        field = jnp.concatenate([ref[half * rows : (half + 1) * rows, :] for ref in messages], axis=0)
        high, middle, low = three_parts(field)
        chosen[:, half * LANES : (half + 1) * LANES] = dot(hot, high) + dot(hot, middle) + dot(hot, low)


def finish(ways, refs):
    sums = refs[:ways]
    zed, you, chosen, drop, sense = refs[ways:]
    total = sums[0][...]
    for ref in sums[1:]:
        total = total + ref[...]
    total = jnp.broadcast_to(jnp.sum(total, axis=1, keepdims=True), (SUB, LANES))
    for which in range(2):
        bz, zq, qu, uw = (total[4 * which + i : 4 * which + i + 1] for i in range(4))
        ratio = qu / zq
        step = bz / zq
        left = uw - ratio * qu
        second = jnp.where(left > 2e-7 * uw, (zq - ratio * bz) / left, -step)
        first = step - second * ratio
        if which == 0:
            for p in range(you.shape[0]):
                part = second * you[p]
                drop[p] = first * zed[p] + part if p < zed.shape[0] else part
        else:
            sense[...] = first * chosen[:, 0:LANES] + second * chosen[:, LANES:]


def vmem():
    return pl.BlockSpec(memory_space=pltpu.VMEM)


def call(kernel, outs, args, scratch=(), specs=None, flops=0, spare=16384):
    size = sum(a.size * a.dtype.itemsize for a in list(args) + list(outs))
    return pl.pallas_call(
        kernel,
        out_shape=tuple(outs),
        in_specs=specs or [vmem() for _ in args],
        out_specs=tuple(vmem() for _ in outs),
        scratch_shapes=scratch,
        cost_estimate=pl.CostEstimate(flops=flops, bytes_accessed=size, transcendentals=0),
        compiler_params=pltpu.CompilerParams(vmem_limit_bytes=(64 * 1024 - spare) * 1024),
    )(*args)


def exchange(values, axis):
    plan = rounds(lax.axis_index(axis), lax.axis_size(axis))
    return [
        lax.ppermute(value, axis, list(enumerate(target)))
        for value, (target, _, _) in zip(values, plan)
    ]


def body(cell_current, block_row, block_count, cond_x, cond_y, cond_via, ground, drop_weight):
    blocks, width = cell_current.shape
    layers, rows, _ = cond_x.shape
    count, ways = lax.axis_size("tx"), lax.axis_size("ty")
    ring = rows + 2 * HALO
    shape = (rows, ring)
    fields = (cond_x, cond_y, cond_via, ground, drop_weight)
    planes = sum(f.shape[0] for f in fields)
    block_row = block_row.reshape(1, blocks)
    hbm = pl.BlockSpec(memory_space=pltpu.HBM)

    def array(*dims, dtype=F32):
        return jax.ShapeDtypeStruct(dims, dtype)

    edges = (planes + 1) // 2 * SUB
    lengths = [ring + (edges if k < 2 else 0) for k in range(count - 1)]
    held, own, home, *sends = call(
        lambda *refs: begin(count, shape, refs),
        [array(planes, rows, LANES), array(ring, LANES), array(1, blocks, dtype=jnp.int32)]
        + [array(n, LANES) for n in lengths],
        (
            *(
                pltpu.with_memory_space_constraint(f, pltpu.HBM)
                for f in (*fields, cell_current, block_row)
            ),
            block_count,
        ),
        scratch=[
            pltpu.VMEM((blocks, LANES), F32),
            pltpu.VMEM((count * ring, blocks), F32),
            pltpu.VMEM((1, blocks), jnp.int32),
            pltpu.SemaphoreType.DMA((len(fields) + 2,)),
        ],
        specs=[hbm] * 7 + [pl.BlockSpec(memory_space=pltpu.SMEM)],
    )
    got = exchange(sends, "tx")
    (chooser,) = call(
        functools.partial(order, count, rows),
        (array(blocks, count * rows, dtype=BF16),),
        (home,),
    )
    packed = array(pl.cdiv(planes * (rows // SUB + 1) + ring // SUB, SLOTS) * SUB, LANES)
    middle, rims, *sends = call(
        lambda *refs: columns(count, shape, refs),
        (array(ring, LANES), array(planes, SUB, LANES), packed, packed),
        (held, own, *in_turn(got, ROW_TURNS)),
    )
    even, odd = exchange(sends, "ty")
    results = (array(min(2, layers), rows, LANES), array(layers, rows, LANES), array(SUB, LANES))
    front, zed, you, total, strips = call(
        lambda *refs: inner(layers, shape, refs),
        (array(2, rows, LANES), *results, array(6, ring, LANES)),
        (held, rims, middle),
        scratch=[
            pltpu.VMEM((8 * layers - 1, ring, LANES), F32),
            pltpu.VMEM((layers, ring, LANES), F32),
        ],
    )
    message, zed, you, total = call(
        lambda *refs: outer(layers, shape, refs),
        (array(2 * rows + SUB, LANES), *results),
        (strips, even, odd, front, zed, you, total),
        scratch=[pltpu.VMEM((6, ring, LANES), F32)],
    )
    got = exchange([message] * (count - 1), "tx")
    ahead = exchange([total] * (count - 1), "tx")[2:]
    total = functools.reduce(jnp.add, [total] + [m[2 * rows :] for m in got[:2]] + ahead)
    messages = in_turn(got, DATA_TURNS) + [message]
    totals = [total] + exchange([total] * (ways - 1), "ty")
    (chosen,) = call(
        lambda *refs: choose(count, rows, refs),
        (array(blocks, 2 * LANES),),
        (chooser, *messages),
    )
    return call(
        lambda *refs: finish(ways, refs),
        (array(layers, rows, LANES), array(blocks, width)),
        (*totals, zed, you, chosen),
    )


def solution(mesh):
    placed = (
        P(("grp", "tx"), "ty"),
        P(("grp", "tx")),
        P(("grp", "tx")),
        P(None, ("grp", "tx"), "ty"),
        P(None, ("grp", "tx"), "ty"),
        P(None, ("grp", "tx"), "ty"),
        P(None, ("grp", "tx"), "ty"),
        P(None, ("grp", "tx"), "ty"),
    )
    return jax.shard_map(
        body,
        mesh=mesh,
        in_specs=placed,
        out_specs=(P(None, ("grp", "tx"), "ty"), P(("grp", "tx"), "ty")),
        check_vma=False,
    )
```

```python
import functools

import jax
import jax.numpy as jnp
from jax import lax
from jax.experimental import pallas as pl
from jax.experimental.pallas import tpu as pltpu
from jax.sharding import PartitionSpec as P

HALO = 4
SUB = 8
LANES = 128
SLOTS = LANES // HALO
WINDOW = 8 * HALO
SHARE = WINDOW // HALO
F32 = jnp.float32
BF16 = jnp.bfloat16
ROW_TURNS = (1, 0, 2)
DATA_TURNS = (1, 0, 2)


def lanes_of(shape):
    return lax.broadcasted_iota(jnp.int32, shape, len(shape) - 1)


def rows_of(shape):
    return lax.broadcasted_iota(jnp.int32, shape, len(shape) - 2)


def strip_kinds(layers):
    depths = (layers, layers, layers - 1, layers, layers)
    return [(sum(depths[:k]), depth) for k, depth in enumerate(depths)] + [(None, 1)]


def strip_tiles(layers, ring):
    groups = [(*kind, at) for kind in strip_kinds(layers) for at in range(0, ring, SUB)]
    return [(k // SHARE * SUB, groups[k : k + SHARE]) for k in range(0, len(groups), SHARE)]


def three_parts(value):
    high = value.astype(BF16)
    rest = value - high.astype(F32)
    middle = rest.astype(BF16)
    low = (rest - middle.astype(F32)).astype(BF16)
    return high, middle, low


def dot(left, right):
    return jnp.dot(left, right, preferred_element_type=F32)


def in_turn(values, turns, back=False):
    turns = turns + tuple(range(len(turns), len(values)))
    if back:
        turns = tuple(turns.index(k) for k in range(len(values)))
    return [values[k] for k in turns]


def rounds(index, count):
    even = [(i + 1) % count if i % 2 == 0 else (i - 1) % count for i in range(count)]
    odd = [(i - 1) % count if i % 2 == 0 else (i + 1) % count for i in range(count)]
    is_even = lax.rem(index, 2) == 0
    up, down = lax.rem(index + 1, count), lax.rem(index + count - 1, count)
    plan = [
        (even, jnp.where(is_even, up, down), jnp.where(is_even, up, down)),
        (odd, jnp.where(is_even, down, up), jnp.where(is_even, down, up)),
    ]
    for k in range(2, count - 1):
        target = [(i + k) % count for i in range(count)]
        plan.append((target, lax.rem(index + k, count), lax.rem(index - k + count, count)))
    return plan


def begin(count, shape, refs):
    fields, cell_in, row_in, block_count = refs[:5], refs[5], refs[6], refs[7]
    planes, own, home = refs[8:11]
    sends = refs[11 : 11 + count - 1]
    cell, picker, block_row, sems = refs[11 + count - 1 :]
    rows, ring = shape
    fetch_row = pltpu.make_async_copy(row_in, block_row, sems.at[6])
    fetch_row.start()
    fetch_cell = pltpu.make_async_copy(cell_in, cell, sems.at[0])
    fetch_cell.start()
    fetches, at = [], 0
    for i, ref in enumerate(fields):
        part = planes.at[at : at + ref.shape[0]]
        fetches.append(pltpu.make_async_copy(ref, part, sems.at[i + 1]))
        fetches[-1].start()
        at += ref.shape[0]

    me = lax.axis_index("tx")
    even = lax.rem(me, 2) == 0
    blocks = block_row.shape[1]
    line = rows_of((ring, blocks))
    line = jnp.where(line < rows + HALO, line, line - ring)
    fetch_row.wait()
    live = lanes_of((1, blocks)) < block_count[0]
    land = jnp.where(live, block_row[...], -rows)
    home[...] = land
    targets = [me] + [target for _, target, _ in rounds(me, count)]
    for k, target in enumerate(targets):
        picker[k * ring : (k + 1) * ring, :] = (line == land - target * rows).astype(F32)
    hot = picker[...].astype(BF16)
    fetch_cell.wait()
    high, middle, low = three_parts(cell[...])
    wide = dot(hot, jnp.concatenate([high, middle, low], axis=1))
    sums = wide[:, 0:LANES] + wide[:, LANES : 2 * LANES] + wide[:, 2 * LANES :]
    own[...] = sums[0:ring]
    for k, send in enumerate(sends):
        send[0:ring, :] = sums[(k + 1) * ring : (k + 2) * ring]

    for fetch in fetches:
        fetch.wait()
    lower = rows_of((SUB, LANES)) < HALO
    for p in range(0, planes.shape[0], 2):
        first = planes[p, 0:SUB, :]
        last = planes[p, rows - SUB : rows, :]
        if p + 1 < planes.shape[0]:
            first = jnp.where(lower, first, pltpu.roll(planes[p + 1, 0:SUB, :], HALO, 0))
            last = jnp.where(lower, pltpu.roll(planes[p + 1, rows - SUB : rows, :], HALO, 0), last)
        at = ring + p // 2 * SUB
        sends[0][at : at + SUB, :] = jnp.where(even, last, first)
        sends[1][at : at + SUB, :] = jnp.where(even, first, last)


def order(count, rows, home, chooser):
    me = lax.axis_index("tx")
    blocks = home.shape[1]
    line = rows_of((rows, blocks))
    for k, source in enumerate(in_turn([source for _, _, source in rounds(me, count)], DATA_TURNS) + [me]):
        hot = (line == home[...] - source * rows).astype(F32)
        chooser[:, k * rows : (k + 1) * rows] = hot.T.astype(BF16)


def columns(count, layers, shape, refs):
    planes, own = refs[:2]
    got = in_turn(refs[2 : 2 + count - 1], ROW_TURNS, True)
    base, rims, send_even, send_odd = refs[2 + count - 1 :]
    rows, ring = shape
    tx_even = lax.rem(lax.axis_index("tx"), 2) == 0
    ty_even = lax.rem(lax.axis_index("ty"), 2) == 0
    lower = rows_of((SUB, LANES)) < HALO
    for i in range(0, ring, SUB):
        total = own[i : i + SUB, :]
        for ref in got:
            total = total + ref[i : i + SUB, :]
        base[i : i + SUB, :] = total
    for p in range(0, planes.shape[0], 2):
        at = ring + p // 2 * SUB
        one, two = got[0][at : at + SUB, :], got[1][at : at + SUB, :]
        after = jnp.where(tx_even, one, two)
        before = jnp.where(tx_even, two, one)
        rims[p] = jnp.where(lower, after, before)
        if p + 1 < planes.shape[0]:
            rims[p + 1] = pltpu.roll(jnp.where(lower, before, after), HALO, 0)

    slot = lanes_of((SUB, LANES)) // HALO
    for q, members in strip_tiles(layers, ring):
        left = jnp.zeros((SUB, LANES), F32)
        right = left
        for k, (first, depth, at) in enumerate(members):
            for p in range(depth):
                if first is None:
                    tile = base[at : at + SUB, :]
                elif at < rows:
                    tile = planes[first + p, at : at + SUB, :]
                else:
                    tile = rims[first + p]
                s = p * SHARE + k
                turned = pltpu.roll(tile, HALO * s, 1) if s else tile
                left = jnp.where(slot == s, turned, left)
                right = jnp.where(slot == (s - 1) % SLOTS, turned, right)
        send_even[q : q + SUB, :] = jnp.where(ty_even, right, left)
        send_odd[q : q + SUB, :] = jnp.where(ty_even, left, right)


class Grid:
    def __init__(self, ref, layers, rows):
        self.layers, self.rows = layers, rows
        self.ring, self.width = ref.shape[1:]
        names = ("cx", "cy", "via", "cx_low", "cy_low", "diagonal", "inverse", "weight")
        at = 0
        for name in names:
            depth = layers - 1 if name == "via" else layers
            setattr(self, name, [ref.at[at + p] for p in range(depth)])
            at += depth
        self.planes = at

    def below(self, v):
        return pltpu.roll(v, self.ring - 1, 0)

    def above(self, v):
        return pltpu.roll(v, 1, 0)

    def right(self, v):
        return pltpu.roll(v, self.width - 1, 1)

    def left(self, v):
        return pltpu.roll(v, 1, 1)

    def couple(self, v, p):
        total = None
        if v[p] is not None:
            total = (
                self.cx[p][...] * self.below(v[p])
                + self.cx_low[p][...] * self.above(v[p])
                + self.cy[p][...] * self.right(v[p])
                + self.cy_low[p][...] * self.left(v[p])
            )
        if p + 1 < self.layers and v[p + 1] is not None:
            term = self.via[p][...] * v[p + 1]
            total = term if total is None else total + term
        if p > 0 and v[p - 1] is not None:
            term = self.via[p - 1][...] * v[p - 1]
            total = term if total is None else total + term
        return total

    def smooth(self, b):
        scaled = [None if v is None else self.inverse[p][...] * v for p, v in enumerate(b)]
        result = []
        for p in range(self.layers):
            total = self.couple(scaled, p)
            if total is not None:
                if b[p] is not None:
                    total = total + b[p]
                total = self.inverse[p][...] * total
            result.append(total)
        return result

    def apply(self, z):
        result = []
        for p in range(self.layers):
            term = self.couple(z, p)
            if z[p] is not None:
                term = self.diagonal[p][...] * z[p] - term
            elif term is not None:
                term = -term
            result.append(term)
        return result

    def flow(self, u):
        result = []
        for p in range(self.layers):
            term = self.cx[p][...] * self.below(u[p]) + self.cy[p][...] * self.right(u[p])
            if p + 1 < self.layers:
                term = term + self.via[p][...] * u[p + 1]
            result.append(self.diagonal[p][...] * u[p] - 2.0 * term)
        return result

    def products(self, b, z, q, u, kept):
        flow = self.flow(u)
        found = []
        for one, two in ((b, z), (z, q), (q, u), (u, flow)):
            total = None
            for left, right in zip(one, two):
                if left is None or right is None:
                    continue
                term = left[0 : self.rows, 0:LANES] * right[0 : self.rows, 0:LANES]
                total = term if total is None else total + term
            found.append(jnp.sum(jnp.where(kept, total, 0.0), axis=0, keepdims=True))
        return found


def inner(layers, shape, refs):
    planes, rims, middle, front, zed, you, sums, strips, grid, ground = refs
    rows, ring = shape
    tx = lax.axis_index("tx")
    op = Grid(grid, layers, rows)
    targets = [*op.cx, *op.cy, *op.via, *(ground.at[p] for p in range(layers)), *op.weight]
    for p, target in enumerate(targets):
        target[0:rows, :] = planes[p]
        target[rows:ring, :] = rims[p]

    row = rows_of((ring, LANES))
    inside = ((row < rows) | (row >= rows + HALO) | (tx < lax.axis_size("tx") - 1)) & (
        (row < rows + HALO) | (tx > 0)
    )
    for p in range(layers):
        cx, cy = op.cx[p][...], op.cy[p][...]
        cx_low = jnp.where((row == 0) & (tx == 0), 0.0, op.above(cx))
        cy_low = op.left(cy)
        total = ground[p] + cx + cx_low + cy + cy_low
        if p + 1 < layers:
            total = total + op.via[p][...]
        if p > 0:
            total = total + op.via[p - 1][...]
        op.cx_low[p][...] = cx_low
        op.cy_low[p][...] = cy_low
        op.diagonal[p][...] = total
        op.inverse[p][...] = jnp.where(inside, 1.0 / total, 0.0)

    lane = lanes_of((rows, LANES))
    kept = (lane >= HALO) & (lane < LANES - HALO)
    b = [ref[...] for ref in op.weight]
    z = op.smooth(b)
    q = op.apply(z)
    u = op.smooth(q)
    front[0] = z[0][0:rows]
    front[1] = u[0][0:rows]
    found = op.products(b, z, q, u, kept)
    b = [middle[...]] + [None] * (layers - 1)
    z = op.smooth(b)
    q = op.apply(z)
    u = op.smooth(q)
    for p in range(layers):
        if z[p] is not None:
            zed[p] = z[p][0:rows]
        you[p] = u[p][0:rows]
    sums[...] = jnp.concatenate(op.products(b, z, q, u, kept) + found, axis=0)

    lane = lanes_of((ring, LANES))
    grounds = [ground.at[p] for p in range(layers)]
    for kind, refs_ in enumerate((op.cx, op.cy, op.via, grounds, op.weight, [middle])):
        packed = jnp.zeros((ring, LANES), F32)
        for p, ref in enumerate(refs_):
            at = p * WINDOW
            first = pltpu.roll(ref[...], at + HALO, 1)
            last = pltpu.roll(ref[...], (at + WINDOW - HALO) % LANES, 1)
            packed = jnp.where((lane >= at + HALO) & (lane < at + WINDOW // 2), first, packed)
            packed = jnp.where((lane >= at + WINDOW // 2) & (lane < at + WINDOW - HALO), last, packed)
        strips[kind] = packed


def outer(layers, shape, refs):
    strips, even, odd, front, zed_in, you_in, sums, message, zed, you, scalars, held = refs
    rows, ring = shape
    tx, ty = lax.axis_index("tx"), lax.axis_index("ty")
    ty_even = lax.rem(ty, 2) == 0

    kinds = strip_kinds(layers)
    lane = lax.rem(lanes_of((SUB, LANES)), WINDOW)
    for q, members in strip_tiles(layers, ring):
        one, two = even[q : q + SUB, :], odd[q : q + SUB, :]
        after, before = jnp.where(ty_even, one, two), jnp.where(ty_even, two, one)
        for k, (first, depth, at) in enumerate(members):
            kind = kinds.index((first, depth))
            part = strips[kind, at : at + SUB, :]
            part = jnp.where(lane < HALO, pltpu.roll(before, (HALO - HALO * k) % LANES, 1), part)
            turned = pltpu.roll(after, (WINDOW - HALO - HALO * k) % LANES, 1)
            held[kind, at : at + SUB, :] = jnp.where(lane >= WINDOW - HALO, turned, part)
    cx, cy, via, ground, weight, source = (held[kind] for kind in range(len(kinds)))

    def below(v):
        return pltpu.roll(v, ring - 1, 0)

    def right(v):
        return pltpu.roll(v, LANES - 1, 1)

    def upper(v):
        return pltpu.roll(v, LANES - WINDOW, 1)

    row, lane = rows_of((ring, LANES)), lax.rem(lanes_of((ring, LANES)), WINDOW)
    inside = (
        ((row < rows) | (row >= rows + HALO) | (tx < lax.axis_size("tx") - 1))
        & ((row < rows + HALO) | (tx > 0))
        & ((lane < WINDOW - HALO) | (ty < lax.axis_size("ty") - 1))
        & ((lane >= HALO) | (ty > 0))
    )
    cx_low = jnp.where((row == 0) & (tx == 0), 0.0, pltpu.roll(cx, 1, 0))
    cy_low = jnp.where((lane == HALO) & (ty == 0), 0.0, pltpu.roll(cy, 1, 1))
    via_low = pltpu.roll(via, WINDOW, 1)
    diagonal = ground + cx + cx_low + cy + cy_low + via + via_low
    inverse = jnp.where(inside, 1.0 / diagonal, 0.0)

    def couple(v):
        return (
            cx * below(v)
            + cx_low * pltpu.roll(v, 1, 0)
            + cy * right(v)
            + cy_low * pltpu.roll(v, 1, 1)
            + via * upper(v)
            + via_low * pltpu.roll(v, WINDOW, 1)
        )

    def smooth(b):
        return inverse * (b + couple(inverse * b))

    near = lane[0:rows]
    near = ((near >= HALO) & (near < 2 * HALO)) | (
        (near >= WINDOW - 2 * HALO) & (near < WINDOW - HALO)
    )
    column = lanes_of((rows, LANES))

    def whole(middle_part, side, p):
        first = pltpu.roll(side[0:rows], (LANES - HALO - p * WINDOW) % LANES, 1)
        last = pltpu.roll(side[0:rows], (LANES + HALO - (p + 1) * WINDOW) % LANES, 1)
        return jnp.where(
            column < HALO, first, jnp.where(column >= LANES - HALO, last, middle_part)
        )

    found = []
    for which, b in enumerate((source, weight)):
        z = smooth(b)
        q = diagonal * z - couple(z)
        u = smooth(q)
        flow = diagonal * u - 2.0 * (cx * below(u) + cy * right(u) + via * upper(u))
        for one, two in ((b, z), (z, q), (q, u), (u, flow)):
            term = jnp.where(near, one[0:rows] * two[0:rows], 0.0)
            found.append(jnp.sum(term, axis=0, keepdims=True))
        if which == 0:
            for p in range(layers):
                if p < zed.shape[0]:
                    zed[p] = whole(zed_in[p], z, p)
                you[p] = whole(you_in[p], u, p)
        else:
            message[0:rows, :] = whole(front[0], z, 0)
            message[rows : 2 * rows, :] = whole(front[1], u, 0)
    found = sums[...] + jnp.concatenate(found, axis=0)
    scalars[...] = found
    message[2 * rows :, :] = found


def choose(count, rows, refs):
    chooser = refs[0]
    messages = refs[1 : 1 + count]
    chosen = refs[1 + count]
    hot = chooser[...]
    for half in range(2):
        field = jnp.concatenate([ref[half * rows : (half + 1) * rows, :] for ref in messages], axis=0)
        high, middle, low = three_parts(field)
        chosen[:, half * LANES : (half + 1) * LANES] = dot(hot, high) + dot(hot, middle) + dot(hot, low)


def finish(ways, refs):
    sums = refs[:ways]
    zed, you, chosen, drop, sense = refs[ways:]
    total = sums[0][...]
    for ref in sums[1:]:
        total = total + ref[...]
    total = jnp.broadcast_to(jnp.sum(total, axis=1, keepdims=True), (SUB, LANES))
    for which in range(2):
        bz, zq, qu, uw = (total[4 * which + i : 4 * which + i + 1] for i in range(4))
        ratio = qu / zq
        step = bz / zq
        left = uw - ratio * qu
        second = jnp.where(left > 2e-7 * uw, (zq - ratio * bz) / left, -step)
        first = step - second * ratio
        if which == 0:
            for p in range(you.shape[0]):
                part = second * you[p]
                drop[p] = first * zed[p] + part if p < zed.shape[0] else part
        else:
            sense[...] = first * chosen[:, 0:LANES] + second * chosen[:, LANES:]


def vmem():
    return pl.BlockSpec(memory_space=pltpu.VMEM)


def call(kernel, outs, args, scratch=(), specs=None, flops=0, spare=16384):
    size = sum(a.size * a.dtype.itemsize for a in list(args) + list(outs))
    return pl.pallas_call(
        kernel,
        out_shape=tuple(outs),
        in_specs=specs or [vmem() for _ in args],
        out_specs=tuple(vmem() for _ in outs),
        scratch_shapes=scratch,
        cost_estimate=pl.CostEstimate(flops=flops, bytes_accessed=size, transcendentals=0),
        compiler_params=pltpu.CompilerParams(vmem_limit_bytes=(64 * 1024 - spare) * 1024),
    )(*args)


def exchange(values, axis):
    plan = rounds(lax.axis_index(axis), lax.axis_size(axis))
    return [
        lax.ppermute(value, axis, list(enumerate(target)))
        for value, (target, _, _) in zip(values, plan)
    ]


def body(cell_current, block_row, block_count, cond_x, cond_y, cond_via, ground, drop_weight):
    blocks, width = cell_current.shape
    layers, rows, _ = cond_x.shape
    count, ways = lax.axis_size("tx"), lax.axis_size("ty")
    ring = rows + 2 * HALO
    shape = (rows, ring)
    fields = (cond_x, cond_y, cond_via, ground, drop_weight)
    planes = sum(f.shape[0] for f in fields)
    block_row = block_row.reshape(1, blocks)
    hbm = pl.BlockSpec(memory_space=pltpu.HBM)

    def array(*dims, dtype=F32):
        return jax.ShapeDtypeStruct(dims, dtype)

    edges = (planes + 1) // 2 * SUB
    lengths = [ring + (edges if k < 2 else 0) for k in range(count - 1)]
    held, own, home, *sends = call(
        lambda *refs: begin(count, shape, refs),
        [array(planes, rows, LANES), array(ring, LANES), array(1, blocks, dtype=jnp.int32)]
        + [array(n, LANES) for n in lengths],
        (
            *(
                pltpu.with_memory_space_constraint(f, pltpu.HBM)
                for f in (*fields, cell_current, block_row)
            ),
            block_count,
        ),
        scratch=[
            pltpu.VMEM((blocks, LANES), F32),
            pltpu.VMEM((count * ring, blocks), F32),
            pltpu.VMEM((1, blocks), jnp.int32),
            pltpu.SemaphoreType.DMA((len(fields) + 2,)),
        ],
        specs=[hbm] * 7 + [pl.BlockSpec(memory_space=pltpu.SMEM)],
    )
    got = exchange(sends, "tx")
    (chooser,) = call(
        functools.partial(order, count, rows),
        (array(blocks, count * rows, dtype=BF16),),
        (home,),
    )
    packed = array(strip_tiles(layers, ring)[-1][0] + SUB, LANES)
    middle, rims, *sends = call(
        lambda *refs: columns(count, layers, shape, refs),
        (array(ring, LANES), array(planes, SUB, LANES), packed, packed),
        (held, own, *in_turn(got, ROW_TURNS)),
    )
    even, odd = exchange(sends, "ty")
    results = (array(min(2, layers), rows, LANES), array(layers, rows, LANES), array(SUB, LANES))
    front, zed, you, total, strips = call(
        lambda *refs: inner(layers, shape, refs),
        (array(2, rows, LANES), *results, array(6, ring, LANES)),
        (held, rims, middle),
        scratch=[
            pltpu.VMEM((8 * layers - 1, ring, LANES), F32),
            pltpu.VMEM((layers, ring, LANES), F32),
        ],
    )
    message, zed, you, total = call(
        lambda *refs: outer(layers, shape, refs),
        (array(2 * rows + SUB, LANES), *results),
        (strips, even, odd, front, zed, you, total),
        scratch=[pltpu.VMEM((6, ring, LANES), F32)],
    )
    got = exchange([message] * (count - 1), "tx")
    ahead = exchange([total] * (count - 1), "tx")[2:]
    total = functools.reduce(jnp.add, ahead + [m[2 * rows :] for m in got[1::-1]] + [total])
    messages = in_turn(got, DATA_TURNS) + [message]
    totals = [total] + exchange([total] * (ways - 1), "ty")
    (chosen,) = call(
        lambda *refs: choose(count, rows, refs),
        (array(blocks, 2 * LANES),),
        (chooser, *messages),
    )
    return call(
        lambda *refs: finish(ways, refs),
        (array(layers, rows, LANES), array(blocks, width)),
        (*totals, zed, you, chosen),
    )


def solution(mesh):
    placed = (
        P(("grp", "tx"), "ty"),
        P(("grp", "tx")),
        P(("grp", "tx")),
        P(None, ("grp", "tx"), "ty"),
        P(None, ("grp", "tx"), "ty"),
        P(None, ("grp", "tx"), "ty"),
        P(None, ("grp", "tx"), "ty"),
        P(None, ("grp", "tx"), "ty"),
    )
    return jax.shard_map(
        body,
        mesh=mesh,
        in_specs=placed,
        out_specs=(P(None, ("grp", "tx"), "ty"), P(("grp", "tx"), "ty")),
        check_vma=False,
    )
```

```python
import functools

import jax
import jax.numpy as jnp
from jax import lax
from jax.experimental import pallas as pl
from jax.experimental.pallas import tpu as pltpu
from jax.sharding import PartitionSpec as P

HALO = 4
SUB = 8
LANES = 128
SLOTS = LANES // HALO
WINDOW = 8 * HALO
SHARE = WINDOW // HALO
F32 = jnp.float32
BF16 = jnp.bfloat16
ROW_TURNS = (1, 0, 2)
DATA_TURNS = (1, 0, 2)


def lanes_of(shape):
    return lax.broadcasted_iota(jnp.int32, shape, len(shape) - 1)


def rows_of(shape):
    return lax.broadcasted_iota(jnp.int32, shape, len(shape) - 2)


def strip_kinds(layers):
    depths = (layers, layers, layers - 1, layers, layers)
    return [(sum(depths[:k]), depth) for k, depth in enumerate(depths)] + [(None, 1)]


def strip_tiles(layers, ring):
    groups = [(*kind, at) for kind in strip_kinds(layers) for at in range(0, ring, SUB)]
    return [(k // SHARE * SUB, groups[k : k + SHARE]) for k in range(0, len(groups), SHARE)]


def three_parts(value):
    high = value.astype(BF16)
    rest = value - high.astype(F32)
    middle = rest.astype(BF16)
    low = (rest - middle.astype(F32)).astype(BF16)
    return high, middle, low


def dot(left, right):
    return jnp.dot(left, right, preferred_element_type=F32)


def in_turn(values, turns, back=False):
    turns = turns + tuple(range(len(turns), len(values)))
    if back:
        turns = tuple(turns.index(k) for k in range(len(values)))
    return [values[k] for k in turns]


def rounds(index, count):
    even = [(i + 1) % count if i % 2 == 0 else (i - 1) % count for i in range(count)]
    odd = [(i - 1) % count if i % 2 == 0 else (i + 1) % count for i in range(count)]
    is_even = lax.rem(index, 2) == 0
    up, down = lax.rem(index + 1, count), lax.rem(index + count - 1, count)
    plan = [
        (even, jnp.where(is_even, up, down), jnp.where(is_even, up, down)),
        (odd, jnp.where(is_even, down, up), jnp.where(is_even, down, up)),
    ]
    for k in range(2, count - 1):
        target = [(i + k) % count for i in range(count)]
        plan.append((target, lax.rem(index + k, count), lax.rem(index - k + count, count)))
    return plan


def begin(count, shape, refs):
    fields, cell_in, row_in, block_count = refs[:5], refs[5], refs[6], refs[7]
    planes, own, home = refs[8:11]
    sends = refs[11 : 11 + count - 1]
    cell, picker, block_row, sems = refs[11 + count - 1 :]
    rows, ring = shape
    fetch_row = pltpu.make_async_copy(row_in, block_row, sems.at[6])
    fetch_row.start()
    fetch_cell = pltpu.make_async_copy(cell_in, cell, sems.at[0])
    fetch_cell.start()
    fetches, at = [], 0
    for i, ref in enumerate(fields):
        part = planes.at[at : at + ref.shape[0]]
        fetches.append(pltpu.make_async_copy(ref, part, sems.at[i + 1]))
        fetches[-1].start()
        at += ref.shape[0]

    me = lax.axis_index("tx")
    even = lax.rem(me, 2) == 0
    blocks = block_row.shape[1]
    line = rows_of((ring, blocks))
    line = jnp.where(line < rows + HALO, line, line - ring)
    fetch_row.wait()
    live = lanes_of((1, blocks)) < block_count[0]
    land = jnp.where(live, block_row[...], -rows)
    home[...] = land
    targets = [me] + [target for _, target, _ in rounds(me, count)]
    for k, target in enumerate(targets):
        picker[k * ring : (k + 1) * ring, :] = (line == land - target * rows).astype(F32)
    hot = picker[...].astype(BF16)
    fetch_cell.wait()
    high, middle, low = three_parts(cell[...])
    wide = dot(hot, jnp.concatenate([high, middle, low], axis=1))
    sums = wide[:, 0:LANES] + wide[:, LANES : 2 * LANES] + wide[:, 2 * LANES :]
    own[...] = sums[0:ring]
    for k, send in enumerate(sends):
        send[0:ring, :] = sums[(k + 1) * ring : (k + 2) * ring]

    for fetch in fetches:
        fetch.wait()
    lower = rows_of((SUB, LANES)) < HALO
    for p in range(0, planes.shape[0], 2):
        first = planes[p, 0:SUB, :]
        last = planes[p, rows - SUB : rows, :]
        if p + 1 < planes.shape[0]:
            first = jnp.where(lower, first, pltpu.roll(planes[p + 1, 0:SUB, :], HALO, 0))
            last = jnp.where(lower, pltpu.roll(planes[p + 1, rows - SUB : rows, :], HALO, 0), last)
        at = ring + p // 2 * SUB
        sends[0][at : at + SUB, :] = jnp.where(even, last, first)
        sends[1][at : at + SUB, :] = jnp.where(even, first, last)


def order(count, rows, home, chooser):
    me = lax.axis_index("tx")
    blocks = home.shape[1]
    line = rows_of((rows, blocks))
    for k, source in enumerate(in_turn([source for _, _, source in rounds(me, count)], DATA_TURNS) + [me]):
        hot = (line == home[...] - source * rows).astype(F32)
        chooser[:, k * rows : (k + 1) * rows] = hot.T.astype(BF16)


def columns(count, layers, shape, refs):
    planes, own = refs[:2]
    got = in_turn(refs[2 : 2 + count - 1], ROW_TURNS, True)
    base, rims, send_even, send_odd = refs[2 + count - 1 :]
    rows, ring = shape
    tx_even = lax.rem(lax.axis_index("tx"), 2) == 0
    ty_even = lax.rem(lax.axis_index("ty"), 2) == 0
    lower = rows_of((SUB, LANES)) < HALO
    for i in range(0, ring, SUB):
        total = own[i : i + SUB, :]
        for ref in got:
            total = total + ref[i : i + SUB, :]
        base[i : i + SUB, :] = total
    for p in range(0, planes.shape[0], 2):
        at = ring + p // 2 * SUB
        one, two = got[0][at : at + SUB, :], got[1][at : at + SUB, :]
        after = jnp.where(tx_even, one, two)
        before = jnp.where(tx_even, two, one)
        rims[p] = jnp.where(lower, after, before)
        if p + 1 < planes.shape[0]:
            rims[p + 1] = pltpu.roll(jnp.where(lower, before, after), HALO, 0)

    slot = lanes_of((SUB, LANES)) // HALO
    for q, members in strip_tiles(layers, ring):
        left = jnp.zeros((SUB, LANES), F32)
        right = left
        for k, (first, depth, at) in enumerate(members):
            for p in range(depth):
                if first is None:
                    tile = base[at : at + SUB, :]
                elif at < rows:
                    tile = planes[first + p, at : at + SUB, :]
                else:
                    tile = rims[first + p]
                s = p * SHARE + k
                turned = pltpu.roll(tile, HALO * s, 1) if s else tile
                left = jnp.where(slot == s, turned, left)
                right = jnp.where(slot == (s - 1) % SLOTS, turned, right)
        send_even[q : q + SUB, :] = jnp.where(ty_even, right, left)
        send_odd[q : q + SUB, :] = jnp.where(ty_even, left, right)


class Grid:
    def __init__(self, ref, layers, rows):
        self.layers, self.rows = layers, rows
        self.ring, self.width = ref.shape[1:]
        names = ("cx", "cy", "via", "cx_low", "cy_low", "diagonal", "inverse", "weight")
        at = 0
        for name in names:
            depth = layers - 1 if name == "via" else layers
            setattr(self, name, [ref.at[at + p] for p in range(depth)])
            at += depth
        self.planes = at

    def below(self, v):
        return pltpu.roll(v, self.ring - 1, 0)

    def above(self, v):
        return pltpu.roll(v, 1, 0)

    def right(self, v):
        return pltpu.roll(v, self.width - 1, 1)

    def left(self, v):
        return pltpu.roll(v, 1, 1)

    def couple(self, v, p):
        total = None
        if v[p] is not None:
            total = (
                self.cx[p][...] * self.below(v[p])
                + self.cx_low[p][...] * self.above(v[p])
                + self.cy[p][...] * self.right(v[p])
                + self.cy_low[p][...] * self.left(v[p])
            )
        if p + 1 < self.layers and v[p + 1] is not None:
            term = self.via[p][...] * v[p + 1]
            total = term if total is None else total + term
        if p > 0 and v[p - 1] is not None:
            term = self.via[p - 1][...] * v[p - 1]
            total = term if total is None else total + term
        return total

    def smooth(self, b):
        scaled = [None if v is None else self.inverse[p][...] * v for p, v in enumerate(b)]
        result = []
        for p in range(self.layers):
            total = self.couple(scaled, p)
            if total is not None:
                if b[p] is not None:
                    total = total + b[p]
                total = self.inverse[p][...] * total
            result.append(total)
        return result

    def apply(self, z):
        result = []
        for p in range(self.layers):
            term = self.couple(z, p)
            if z[p] is not None:
                term = self.diagonal[p][...] * z[p] - term
            elif term is not None:
                term = -term
            result.append(term)
        return result

    def flow(self, u):
        result = []
        for p in range(self.layers):
            term = self.cx[p][...] * self.below(u[p]) + self.cy[p][...] * self.right(u[p])
            if p + 1 < self.layers:
                term = term + self.via[p][...] * u[p + 1]
            result.append(self.diagonal[p][...] * u[p] - 2.0 * term)
        return result

    def products(self, b, z, q, u, kept):
        flow = self.flow(u)
        found = []
        for one, two in ((b, z), (z, q), (q, u), (u, flow)):
            total = None
            for left, right in zip(one, two):
                if left is None or right is None:
                    continue
                term = left[0 : self.rows, 0:LANES] * right[0 : self.rows, 0:LANES]
                total = term if total is None else total + term
            found.append(jnp.sum(jnp.where(kept, total, 0.0), axis=0, keepdims=True))
        return found


def inner(layers, shape, refs):
    planes, rims, middle, front, zed, you, sums, strips, grid, ground = refs
    rows, ring = shape
    tx = lax.axis_index("tx")
    op = Grid(grid, layers, rows)
    targets = [*op.cx, *op.cy, *op.via, *(ground.at[p] for p in range(layers)), *op.weight]
    for p, target in enumerate(targets):
        target[0:rows, :] = planes[p]
        target[rows:ring, :] = rims[p]

    row = rows_of((ring, LANES))
    inside = ((row < rows) | (row >= rows + HALO) | (tx < lax.axis_size("tx") - 1)) & (
        (row < rows + HALO) | (tx > 0)
    )
    for p in range(layers):
        cx, cy = op.cx[p][...], op.cy[p][...]
        cx_low = jnp.where((row == 0) & (tx == 0), 0.0, op.above(cx))
        cy_low = op.left(cy)
        total = ground[p] + cx + cx_low + cy + cy_low
        if p + 1 < layers:
            total = total + op.via[p][...]
        if p > 0:
            total = total + op.via[p - 1][...]
        op.cx_low[p][...] = cx_low
        op.cy_low[p][...] = cy_low
        op.diagonal[p][...] = total
        op.inverse[p][...] = jnp.where(inside, 1.0 / total, 0.0)

    lane = lanes_of((rows, LANES))
    kept = (lane >= HALO) & (lane < LANES - HALO)
    b = [ref[...] for ref in op.weight]
    z = op.smooth(b)
    q = op.apply(z)
    u = op.smooth(q)
    front[0] = z[0][0:rows]
    front[1] = u[0][0:rows]
    found = op.products(b, z, q, u, kept)
    b = [middle[...]] + [None] * (layers - 1)
    z = op.smooth(b)
    q = op.apply(z)
    u = op.smooth(q)
    for p in range(layers):
        if z[p] is not None:
            zed[p] = z[p][0:rows]
        you[p] = u[p][0:rows]
    sums[...] = jnp.concatenate(op.products(b, z, q, u, kept) + found, axis=0)

    lane = lanes_of((ring, LANES))
    grounds = [ground.at[p] for p in range(layers)]
    for kind, refs_ in enumerate((op.cx, op.cy, op.via, grounds, op.weight, [middle])):
        packed = jnp.zeros((ring, LANES), F32)
        for p, ref in enumerate(refs_):
            at = p * WINDOW
            first = pltpu.roll(ref[...], at + HALO, 1)
            last = pltpu.roll(ref[...], (at + WINDOW - HALO) % LANES, 1)
            packed = jnp.where((lane >= at + HALO) & (lane < at + WINDOW // 2), first, packed)
            packed = jnp.where((lane >= at + WINDOW // 2) & (lane < at + WINDOW - HALO), last, packed)
        strips[kind] = packed


def outer(layers, shape, refs):
    strips, even, odd, front, zed_in, you_in, sums, message, zed, you, scalars, held = refs
    rows, ring = shape
    tx, ty = lax.axis_index("tx"), lax.axis_index("ty")
    ty_even = lax.rem(ty, 2) == 0

    kinds = strip_kinds(layers)
    lane = lax.rem(lanes_of((SUB, LANES)), WINDOW)
    for q, members in strip_tiles(layers, ring):
        one, two = even[q : q + SUB, :], odd[q : q + SUB, :]
        after, before = jnp.where(ty_even, one, two), jnp.where(ty_even, two, one)
        for k, (first, depth, at) in enumerate(members):
            kind = kinds.index((first, depth))
            part = strips[kind, at : at + SUB, :]
            part = jnp.where(lane < HALO, pltpu.roll(before, (HALO - HALO * k) % LANES, 1), part)
            turned = pltpu.roll(after, (WINDOW - HALO - HALO * k) % LANES, 1)
            held[kind, at : at + SUB, :] = jnp.where(lane >= WINDOW - HALO, turned, part)
    cx, cy, via, ground, weight, source = (held[kind] for kind in range(len(kinds)))

    def below(v):
        return pltpu.roll(v, ring - 1, 0)

    def right(v):
        return pltpu.roll(v, LANES - 1, 1)

    def upper(v):
        return pltpu.roll(v, LANES - WINDOW, 1)

    row, lane = rows_of((ring, LANES)), lax.rem(lanes_of((ring, LANES)), WINDOW)
    inside = (
        ((row < rows) | (row >= rows + HALO) | (tx < lax.axis_size("tx") - 1))
        & ((row < rows + HALO) | (tx > 0))
        & ((lane < WINDOW - HALO) | (ty < lax.axis_size("ty") - 1))
        & ((lane >= HALO) | (ty > 0))
    )
    cx_low = jnp.where((row == 0) & (tx == 0), 0.0, pltpu.roll(cx, 1, 0))
    cy_low = jnp.where((lane == HALO) & (ty == 0), 0.0, pltpu.roll(cy, 1, 1))
    via_low = pltpu.roll(via, WINDOW, 1)
    diagonal = ground + cx + cx_low + cy + cy_low + via + via_low
    inverse = jnp.where(inside, 1.0 / diagonal, 0.0)

    def couple(v):
        return (
            cx * below(v)
            + cx_low * pltpu.roll(v, 1, 0)
            + cy * right(v)
            + cy_low * pltpu.roll(v, 1, 1)
            + via * upper(v)
            + via_low * pltpu.roll(v, WINDOW, 1)
        )

    def smooth(b):
        return inverse * (b + couple(inverse * b))

    near = lane[0:rows]
    near = ((near >= HALO) & (near < 2 * HALO)) | (
        (near >= WINDOW - 2 * HALO) & (near < WINDOW - HALO)
    )
    column = lanes_of((rows, LANES))

    def whole(middle_part, side, p):
        first = pltpu.roll(side[0:rows], (LANES - HALO - p * WINDOW) % LANES, 1)
        last = pltpu.roll(side[0:rows], (LANES + HALO - (p + 1) * WINDOW) % LANES, 1)
        return jnp.where(
            column < HALO, first, jnp.where(column >= LANES - HALO, last, middle_part)
        )

    bs = (source, weight)
    zs = [smooth(b) for b in bs]
    qs = [diagonal * z - couple(z) for z in zs]
    us = [smooth(q) for q in qs]
    flows = [diagonal * u - 2.0 * (cx * below(u) + cy * right(u) + via * upper(u)) for u in us]
    found = []
    for b, z, q, u, flow in zip(bs, zs, qs, us, flows):
        for one, two in ((b, z), (z, q), (q, u), (u, flow)):
            term = jnp.where(near, one[0:rows] * two[0:rows], 0.0)
            found.append(jnp.sum(term, axis=0, keepdims=True))
    for p in range(layers):
        if p < zed.shape[0]:
            zed[p] = whole(zed_in[p], zs[0], p)
        you[p] = whole(you_in[p], us[0], p)
    message[0:rows, :] = whole(front[0], zs[1], 0)
    message[rows : 2 * rows, :] = whole(front[1], us[1], 0)
    found = sums[...] + jnp.concatenate(found, axis=0)
    scalars[...] = found
    message[2 * rows :, :] = found


def choose(count, rows, refs):
    chooser = refs[0]
    messages = refs[1 : 1 + count]
    chosen = refs[1 + count]
    hot = chooser[...]
    for half in range(2):
        field = jnp.concatenate([ref[half * rows : (half + 1) * rows, :] for ref in messages], axis=0)
        high, middle, low = three_parts(field)
        chosen[:, half * LANES : (half + 1) * LANES] = dot(hot, high) + dot(hot, middle) + dot(hot, low)


def finish(ways, refs):
    sums = refs[:ways]
    zed, you, chosen, drop, sense = refs[ways:]
    total = sums[0][...]
    for ref in sums[1:]:
        total = total + ref[...]
    total = jnp.broadcast_to(jnp.sum(total, axis=1, keepdims=True), (SUB, LANES))
    for which in range(2):
        bz, zq, qu, uw = (total[4 * which + i : 4 * which + i + 1] for i in range(4))
        ratio = qu / zq
        step = bz / zq
        left = uw - ratio * qu
        second = jnp.where(left > 2e-7 * uw, (zq - ratio * bz) / left, -step)
        first = step - second * ratio
        if which == 0:
            for p in range(you.shape[0]):
                part = second * you[p]
                drop[p] = first * zed[p] + part if p < zed.shape[0] else part
        else:
            sense[...] = first * chosen[:, 0:LANES] + second * chosen[:, LANES:]


def vmem():
    return pl.BlockSpec(memory_space=pltpu.VMEM)


def call(kernel, outs, args, scratch=(), specs=None, flops=0, spare=16384):
    size = sum(a.size * a.dtype.itemsize for a in list(args) + list(outs))
    return pl.pallas_call(
        kernel,
        out_shape=tuple(outs),
        in_specs=specs or [vmem() for _ in args],
        out_specs=tuple(vmem() for _ in outs),
        scratch_shapes=scratch,
        cost_estimate=pl.CostEstimate(flops=flops, bytes_accessed=size, transcendentals=0),
        compiler_params=pltpu.CompilerParams(vmem_limit_bytes=(64 * 1024 - spare) * 1024),
    )(*args)


def exchange(values, axis):
    plan = rounds(lax.axis_index(axis), lax.axis_size(axis))
    return [
        lax.ppermute(value, axis, list(enumerate(target)))
        for value, (target, _, _) in zip(values, plan)
    ]


def body(cell_current, block_row, block_count, cond_x, cond_y, cond_via, ground, drop_weight):
    blocks, width = cell_current.shape
    layers, rows, _ = cond_x.shape
    count, ways = lax.axis_size("tx"), lax.axis_size("ty")
    ring = rows + 2 * HALO
    shape = (rows, ring)
    fields = (cond_x, cond_y, cond_via, ground, drop_weight)
    planes = sum(f.shape[0] for f in fields)
    block_row = block_row.reshape(1, blocks)
    hbm = pl.BlockSpec(memory_space=pltpu.HBM)

    def array(*dims, dtype=F32):
        return jax.ShapeDtypeStruct(dims, dtype)

    edges = (planes + 1) // 2 * SUB
    lengths = [ring + (edges if k < 2 else 0) for k in range(count - 1)]
    held, own, home, *sends = call(
        lambda *refs: begin(count, shape, refs),
        [array(planes, rows, LANES), array(ring, LANES), array(1, blocks, dtype=jnp.int32)]
        + [array(n, LANES) for n in lengths],
        (
            *(
                pltpu.with_memory_space_constraint(f, pltpu.HBM)
                for f in (*fields, cell_current, block_row)
            ),
            block_count,
        ),
        scratch=[
            pltpu.VMEM((blocks, LANES), F32),
            pltpu.VMEM((count * ring, blocks), F32),
            pltpu.VMEM((1, blocks), jnp.int32),
            pltpu.SemaphoreType.DMA((len(fields) + 2,)),
        ],
        specs=[hbm] * 7 + [pl.BlockSpec(memory_space=pltpu.SMEM)],
    )
    got = exchange(sends, "tx")
    (chooser,) = call(
        functools.partial(order, count, rows),
        (array(blocks, count * rows, dtype=BF16),),
        (home,),
    )
    packed = array(strip_tiles(layers, ring)[-1][0] + SUB, LANES)
    middle, rims, *sends = call(
        lambda *refs: columns(count, layers, shape, refs),
        (array(ring, LANES), array(planes, SUB, LANES), packed, packed),
        (held, own, *in_turn(got, ROW_TURNS)),
    )
    even, odd = exchange(sends, "ty")
    results = (array(min(2, layers), rows, LANES), array(layers, rows, LANES), array(SUB, LANES))
    front, zed, you, total, strips = call(
        lambda *refs: inner(layers, shape, refs),
        (array(2, rows, LANES), *results, array(6, ring, LANES)),
        (held, rims, middle),
        scratch=[
            pltpu.VMEM((8 * layers - 1, ring, LANES), F32),
            pltpu.VMEM((layers, ring, LANES), F32),
        ],
    )
    message, zed, you, total = call(
        lambda *refs: outer(layers, shape, refs),
        (array(2 * rows + SUB, LANES), *results),
        (strips, even, odd, front, zed, you, total),
        scratch=[pltpu.VMEM((6, ring, LANES), F32)],
    )
    got = exchange([message] * (count - 1), "tx")
    ahead = exchange([total] * (count - 1), "tx")[2:]
    total = functools.reduce(jnp.add, ahead + [m[2 * rows :] for m in got[1::-1]] + [total])
    messages = in_turn(got, DATA_TURNS) + [message]
    totals = [total] + exchange([total] * (ways - 1), "ty")
    (chosen,) = call(
        lambda *refs: choose(count, rows, refs),
        (array(blocks, 2 * LANES),),
        (chooser, *messages),
    )
    return call(
        lambda *refs: finish(ways, refs),
        (array(layers, rows, LANES), array(blocks, width)),
        (*totals, zed, you, chosen),
    )


def solution(mesh):
    placed = (
        P(("grp", "tx"), "ty"),
        P(("grp", "tx")),
        P(("grp", "tx")),
        P(None, ("grp", "tx"), "ty"),
        P(None, ("grp", "tx"), "ty"),
        P(None, ("grp", "tx"), "ty"),
        P(None, ("grp", "tx"), "ty"),
        P(None, ("grp", "tx"), "ty"),
    )
    return jax.shard_map(
        body,
        mesh=mesh,
        in_specs=placed,
        out_specs=(P(None, ("grp", "tx"), "ty"), P(("grp", "tx"), "ty")),
        check_vma=False,
    )
```
